512 devices in a mesh: blk: 64 (over x_hi, z, core), tgt: 8 (over x_lo, y).
Axes of the slice: x: 4 (x_hi: 2, x_lo: 2; x = x_hi * 2 + x_lo), y: 4, z: 16, core: 2. Of those that a mesh axis runs over, the one named last changes fastest.
Arguments:
- positions: float32 [3, 65536], P(None, ('blk', 'tgt')), may hold values from -1 to 1
- area: float32 [65536], P(('blk', 'tgt')), may hold values from 0.5 to 2
- density: float32 [2, 65536], P(None, ('blk', 'tgt')), may hold values from -6 to 6
- near_dest: int32 [262144, 1], P(('blk', 'tgt')), may hold values from 0 to 511; in each aligned block of 512 rows (0 to 511, 512 to 1023, ...) at most 2 rows name the same one
- near_offset: int32 [262144], P(('blk', 'tgt')), may hold values from 0 to 127
- near_source: int32 [262144], P(('blk', 'tgt')), may hold values from 0 to 127
- near_order: int32 [262144], P(('blk', 'tgt')), may hold values from 1 to 4
Outputs:
- image: float32 [2, 65536], P(None, ('blk', 'tgt'))
The draws below stay inside these ranges and needn't reach their ends.
Inputs may be any that keep to these rules, and one draw needn't show every extreme that they name: `near_dest`: among the near pairs held by one device, no owner device is named more than 2 times, and one is named exactly 2 times; every device owns the target of some pair.
All inputs are finite; a program needn't handle non-finite values.
Results may differ from the reference program's by a relative error of at most 0.0003.
Values sent between devices are 32-bit elements; how exact they have to be, the bound alone decides.
No kernel may reach another device: no remote copies, remote signals or barrier semaphores. Data moves between devices by JAX's collectives and lax.ppermute only.
A program may use at most 64 MiB of HBM per device.

```python
import math
import jax
import jax.numpy as jnp
import numpy as np
from jax import lax

TT = 128
NEAR_DEV = 512
NP = 65536
NPAIRS = 262144
CAP = 2
N_BLK = 64
N_TGT = 8


def place_ends(values, key, least, largest):
    place = [jax.random.randint(jax.random.fold_in(key, axis), (), 0, length) for axis, length in enumerate(values.shape)]
    longest = values.shape.index(max(values.shape))
    next_to = place[:longest] + [(place[longest] + 1) % values.shape[longest]] + place[longest + 1:]
    return values.at[tuple(place)].set(least).at[tuple(next_to)].set(largest)


def block_scale(stream_key, dims, split, low, largest):
    gain = 1.0
    for position, blocks in split:
        steps = jax.random.uniform(jax.random.fold_in(jax.random.fold_in(stream_key, 6), position), (blocks,), jnp.float32, low / len(split), largest / len(split))
        gain = gain * jnp.repeat(jnp.exp(steps), dims[position] // blocks).reshape((-1,) + (1,) * (len(dims) - 1 - position))
    return gain


def deal_out(rng, own, number, rows, count, top, bound, slope):
    ranking = jax.random.permutation(rng, count)
    heavy_load, ordinary = shares(count, rows * top, bound, slope, True), shares(count, rows * top, bound, slope, False)
    places = jnp.arange(count)

    def named(lengths, offset_by):
        used = int((lengths > 0).sum())
        fixed = max(1, used // 4)
        passed = fixed + (places - fixed + offset_by * (used - fixed)) % max(1, count - fixed)
        return jnp.zeros((count,), jnp.int32).at[ranking[jnp.where(places < fixed, places, passed)]].set(jnp.asarray(lengths, jnp.int32))

    lengths = jnp.where(number % 4 == 0, named(heavy_load, number // 4), named(ordinary, number - number // 4 - 1))
    mixed = jax.random.permutation(jax.random.fold_in(own, 3), count)
    giver, taker = mixed[0:count // 2 * 2:2], mixed[1:count // 2 * 2:2]
    margin = jnp.minimum(lengths[giver] - 1, bound - lengths[taker]) // 2
    margin = jnp.where((giver == ranking[0]) | (taker == ranking[0]) | (lengths[taker] == 0), 0, jnp.maximum(margin, 0))
    passed = jax.random.randint(jax.random.fold_in(own, 4), (count // 2,), 0, 1 << 20) % (margin + 1)
    lengths = lengths.at[giver].add(-passed).at[taker].add(passed)
    labels = jnp.searchsorted(jnp.cumsum(lengths), jnp.arange(rows * top), side="right").astype(jnp.int32)
    grid = labels.reshape(top, rows).T
    grid = grid[jax.random.permutation(jax.random.fold_in(own, 1), rows)]
    offset_by = jax.random.randint(jax.random.fold_in(own, 2), (rows, 1), 0, top)
    return jnp.take_along_axis(grid, (jnp.arange(top)[None, :] + offset_by) % top, axis=1)


def shares(number_of, total, most, slope, full):
    weights = [(1 << 20) // math.isqrt(grade ** slope) + 1 for grade in range(1, number_of + 1)]
    largest = most if full else min(most, max(-(-total // number_of), total * weights[0] // sum(weights)))
    least = 1 if total - largest >= number_of - 1 else 0
    holding, rest = [largest] + [least] * (number_of - 1), total - largest - least * (number_of - 1)
    while rest > 0:
        movable = [i for i in range(1, number_of) if holding[i] < largest] or [i for i in range(1, number_of) if holding[i] < most]
        pool, budget = sum([weights[i] for i in movable]), rest
        for i in movable:
            extra = min(most - holding[i], max(1, budget * weights[i] // pool), rest)
            holding[i] = holding[i] + extra
            rest = rest - extra
    return np.array(holding)


def normal_values(stream_key, shape, width, reach, cuts=(), kind=jnp.bfloat16):
    array = jax.random.normal(stream_key, shape, jnp.float32) * width
    if len(cuts) > 0:
        array = block_scale(stream_key, shape, cuts, -0.22, 0.18) * array
    return jnp.clip(array, min=-reach, max=reach).astype(kind)


def setup_inputs(seed: int = 0) -> dict:
    key_list = jax.random.split(jax.random.key(seed), 8)
    positions = jnp.clip(jax.random.uniform(key_list[0], (3, NP), jnp.float32, -1.0, 1.0) * block_scale(key_list[0], (3, NP), ((1, 512),), -0.4, 0.0), -1.0, 1.0)
    area = jnp.clip(jnp.exp(math.log(2.0) - 1.3862944 * jax.random.uniform(key_list[1], (NP,), jnp.float32) ** block_scale(key_list[1], (NP,), ((0, 512),), -0.2, 0.2)), 0.5, 2.0)
    density = normal_values(key_list[2], (2, NP), 1.0, 6.0, ((1, 512),), jnp.float32)
    near_dest_keys = jax.random.split(jax.random.fold_in(key_list[3], 1), NPAIRS // NEAR_DEV)
    near_dest_turns = jax.random.permutation(jax.random.fold_in(key_list[3], 3), NPAIRS // NEAR_DEV)
    near_dest = jax.vmap(lambda own, number: deal_out(jax.random.fold_in(key_list[3], 2), own, number, NEAR_DEV, N_BLK * N_TGT, 1, CAP, 2))(near_dest_keys, near_dest_turns).reshape((NPAIRS, 1))
    near_offset = place_ends(jax.random.randint(key_list[4], (NPAIRS,), 0, TT), jax.random.fold_in(key_list[4], 1), 0, TT - 1).astype(jnp.int32)
    near_source = place_ends(jax.random.randint(key_list[5], (NPAIRS,), 0, TT), jax.random.fold_in(key_list[5], 1), 0, TT - 1).astype(jnp.int32)
    near_order = place_ends(jax.random.randint(key_list[6], (NPAIRS,), 1, 5), jax.random.fold_in(key_list[6], 1), 1, 4).astype(jnp.int32)
    return {"positions": positions, "area": area, "density": density, "near_dest": near_dest, "near_offset": near_offset, "near_source": near_source, "near_order": near_order}


wave_number = 6.0

def far_tile(target_pos, source_pos, source_area, source_den, panel_total):
    dx = target_pos[0][:, None] - source_pos[0][None, :]
    dy = target_pos[1][:, None] - source_pos[1][None, :]
    dz = target_pos[2][:, None] - source_pos[2][None, :]
    radius_sq = dx * dx + dy * dy + dz * dz
    radius = jnp.sqrt(radius_sq)
    weight = source_area[None, :] / jnp.sqrt(panel_total * 1.0) / jnp.sqrt(radius_sq + source_area[None, :] / panel_total)
    real_part = jnp.cos(wave_number * radius) * weight
    imag_part = jnp.sin(wave_number * radius) * weight
    out_re = lax.optimization_barrier(jnp.sum(real_part * source_den[0][None, :] - imag_part * source_den[1][None, :], axis=1))
    out_im = lax.optimization_barrier(jnp.sum(real_part * source_den[1][None, :] + imag_part * source_den[0][None, :], axis=1))
    return jnp.stack([out_re, out_im], 0)

def near_terms(target_pos, record, order, panel_total):
    delta = target_pos - record[0:3]
    radius_sq = lax.optimization_barrier(jnp.sum(delta * delta, axis=0))
    radius = jnp.sqrt(radius_sq)
    source_area = record[3]
    empty = jnp.where(order > 0, 0.0, 1.0)
    amplitude = 0.25 * order.astype(jnp.float32) * source_area / jnp.sqrt(radius_sq + (source_area + empty) / panel_total)
    real_part = jnp.cos(wave_number * radius) * amplitude
    imag_part = jnp.sin(wave_number * radius) * amplitude
    return jnp.stack([real_part * record[4] - imag_part * record[5], real_part * record[5] + imag_part * record[4]], 0)

def reference(positions, area, density, near_dest, near_offset, near_source, near_order):
    blocks = NP // TT
    target_blocks = positions.reshape(3, blocks, TT).transpose(1, 0, 2)
    source_width = min(NP, 4096)
    source_count = NP // source_width
    source_pos = positions.reshape(3, source_count, source_width).transpose(1, 0, 2)
    source_area = area.reshape(source_count, source_width)
    source_den = density.reshape(2, source_count, source_width).transpose(1, 0, 2)

    def one_block(target_pos):

        def add_source(total, piece):
            return (total + far_tile(target_pos, piece[0], piece[1], piece[2], NP), None)
        start = jnp.zeros((2, TT), jnp.float32)
        total, unused = lax.scan(add_source, start, (source_pos, source_area, source_den))
        return total
    far = lax.map(one_block, target_blocks).transpose(1, 0, 2).reshape(2, NP)
    pair_ids = jnp.arange(NPAIRS, dtype=jnp.int32)
    source_ids = pair_ids // NEAR_DEV * TT + near_source
    target_ids = near_dest[:, 0] * TT + near_offset
    record = jnp.concatenate([positions[:, source_ids], area[source_ids][None, :], density[:, source_ids]], 0)
    terms = near_terms(positions[:, target_ids], record, near_order, NP)
    near_re = jax.ops.segment_sum(terms[0], target_ids, num_segments=NP)
    near_im = jax.ops.segment_sum(terms[1], target_ids, num_segments=NP)
    near = jnp.stack([near_re, near_im], 0)
    return 0.5 * density + far + near
```

```python
import functools
import math

import jax
import jax.numpy as jnp
import numpy as np
from jax import lax
from jax.experimental import pallas as pl
from jax.experimental.pallas import tpu as pltpu
from jax.sharding import Mesh
from jax.sharding import PartitionSpec as P

f32 = jnp.float32
bf16 = jnp.bfloat16
i32 = jnp.int32

AXES = ("xh", "z", "c", "xl", "y")
ROW = ("z",)
COL = ("xh", "c", "xl", "y")
N_ROW, N_COL = 16, 32

TURNS = 6.0 / (2.0 * math.pi)
S1, S3, S5 = 1.57078847, -0.64571199, 0.07766739
B1, B3 = S1 / S5, S3 / S5
ONE = 1.0 / (S5 * S5)
BACK = 8.0 * S5**4

FEATURES = 80
CHUNK = 512
VMEM = pl.BlockSpec(memory_space=pltpu.VMEM)


def wave(s, eps, amp, phase):
    weight = lax.rsqrt(s + eps) * amp
    s = jnp.maximum(s, 1e-30)
    turns = s * lax.rsqrt(s) + phase
    f = turns - jnp.round(turns)
    f2 = f * f
    sine = f * (B1 + f2 * (B3 + f2))
    u = sine * sine
    d = ONE - u
    half_sin = sine * (d * lax.rsqrt(d))
    half_cos = (0.5 * ONE) - u
    part = weight * half_sin
    return weight, part * half_sin, part * half_cos


def prepare_kernel(rec_ref, dest_ref, off_ref, src_ref, ord_ref, msg_ref):
    for z in range(N_ROW):
        msg_ref[z, 0:6, :] = rec_ref[...]
    dest = dest_ref[...]
    pad = jnp.concatenate([dest, dest], 0).astype(f32)
    columns = jnp.transpose(pad).astype(i32)
    sub = lax.broadcasted_iota(i32, (128, 128), 0)
    lane = lax.broadcasted_iota(i32, (128, 128), 1)
    rows16 = lax.broadcasted_iota(i32, (16, 128), 0)
    first = jnp.zeros((16, 128), f32)
    second = jnp.zeros((16, 128), f32)
    nt = (((1,), (1,)), ((), ()))
    for k in range(4):
        row = dest[k : k + 1, :]
        count = jnp.zeros((128, 128), f32)
        for j in range(k + 1):
            same = columns[:, j : j + 1] == row
            if j == k:
                same = same & (sub < lane)
            count = count + jnp.where(same, 1.0, 0.0)
        rank = jnp.sum(count, axis=0, keepdims=True).astype(i32)
        slot = rank * N_COL + (lax.shift_right_logical(row, 8) * 16 + (row & 15))
        layer = lax.shift_right_logical(row, 4) & 15
        mine = layer == rows16
        low = jnp.where(sub == slot, 1.0, 0.0).astype(bf16)
        high = jnp.where(sub == slot + 64, 1.0, 0.0).astype(bf16)

        def values(ref):
            return jnp.where(mine, ref[k : k + 1, :].astype(f32), 0.0).astype(bf16)

        def put(a, b):
            return lax.dot_general(a, b, nt, preferred_element_type=f32)

        first = first + put(values(off_ref), low) + put(values(src_ref), high)
        second = second + put(values(ord_ref), low)
    msg_ref[:, 6, :] = first
    msg_ref[:, 7, :] = second


def split(x):
    h = jnp.round(x * 64.0) * (1.0 / 64.0)
    m = jnp.round((x - h) * 16384.0) * (1.0 / 16384.0)
    l = jnp.round(((x - h) - m) * 8388608.0) * (1.0 / 8388608.0)
    return h, m, l


def norms(h, m, l):
    exact = jnp.sum(h * h + 2.0 * (h * m), axis=0, keepdims=True)
    e1 = jnp.round(exact * 64.0) * (1.0 / 64.0)
    e2 = jnp.round((exact - e1) * 16384.0) * (1.0 / 16384.0)
    e3 = (exact - e1) - e2
    rest = jnp.sum(2.0 * (h * l) + (m * m + (2.0 * (m * l) + l * l)), axis=0, keepdims=True)
    r1 = jnp.round(rest * 524288.0) * (1.0 / 524288.0)
    r2 = jnp.round((rest - r1) * 134217728.0) * (1.0 / 134217728.0)
    r3 = (rest - r1) - r2
    return (e1, e2, e3), (r1, r2, r3)


def assemble(groups, width):
    blocks = []
    for xyz, extra in groups:
        parts = [xyz]
        if extra is None:
            parts.append(jnp.zeros((5, width), f32))
        else:
            parts.extend(extra)
            parts.append(jnp.zeros((2, width), f32))
        blocks.append(jnp.concatenate(parts, 0))
    return jnp.concatenate(blocks, 0)


def source_features(x):
    h, m, l = split(x)
    exact, rest = norms(h, m, l)
    ones = [jnp.ones((1, x.shape[1]), f32)] * 3
    order = [
        (h, exact), (h, ones), (m, None), (m, rest), (h, ones), (l, None), (m, None), (l, None), (l, None),
    ]
    return assemble(order, x.shape[1])


def target_features(x):
    h, m, l = split(x)
    exact, rest = norms(h, m, l)
    ones = [jnp.ones((1, x.shape[1]), f32)] * 3
    h, m, l = -2.0 * h, -2.0 * m, -2.0 * l
    order = [
        (h, ones), (m, exact), (h, None), (m, ones), (l, rest), (h, None), (l, None), (m, None), (l, None),
    ]
    return assemble(order, x.shape[1])


def near_part(tgt_ref, rec_ref, near_re, near_im):
    src = rec_ref[:, 6, :]
    index = pltpu.roll(src, 64, 1).astype(i32)
    index = jnp.clip(index, 0, 127)
    gathered = [jnp.take_along_axis(rec_ref[:, k, :], index, axis=1) for k in range(6)]
    stack = jnp.concatenate(gathered + [src, rec_ref[:, 7, :]], 0)
    turned = jnp.transpose(stack)[0:64, :]
    fields = [turned] + [pltpu.roll(turned, 128 - 16 * k, 1) for k in range(1, 8)]
    offset = jnp.clip(fields[6].astype(i32), 0, 127)
    s = jnp.zeros((64, 128), f32)
    for k in range(3):
        place = tgt_ref[:, k, :]
        place = jnp.concatenate([place, place], 0)
        gap = jnp.take_along_axis(place, offset, axis=1) * TURNS - fields[k] * TURNS
        s = s + gap * gap
    weight, part_re, part_im = wave(s, fields[3], fields[4], fields[5])
    scale = 64.0 * fields[7]
    term_re = scale * (weight - BACK * part_re)
    term_im = scale * (BACK * part_im)
    lane = lax.broadcasted_iota(i32, (64, 128), 1)
    total_re = jnp.zeros((64, 128), f32)
    total_im = jnp.zeros((64, 128), f32)
    for j in range(N_ROW):
        hit = offset[:, j : j + 1] == lane
        total_re = total_re + jnp.where(hit, term_re[:, j : j + 1], 0.0)
        total_im = total_im + jnp.where(hit, term_im[:, j : j + 1], 0.0)
    near_re[...] = total_re[0:32, :] + total_re[32:64, :]
    near_im[...] = total_im[0:32, :] + total_im[32:64, :]


def sum_kernel(tgt_ref, rec_ref, out_ref, src_f, tgt_f, par, near_re, near_im, dist_a, dist_b):
    n_src = N_ROW * 128
    pairs = N_COL // 2

    near_part(tgt_ref, rec_ref, near_re, near_im)

    def source_block(b, carry):
        record = rec_ref[b]
        rows = source_features(record[0:3, :] * TURNS)
        rows = jnp.concatenate([rows, record, jnp.zeros((48, 128), f32)], 0)
        turned = jnp.transpose(rows)
        place = pl.ds(pl.multiple_of(b * 128, 128), 128)
        src_f[place, :] = turned[:, 0:FEATURES].astype(bf16)
        for k in range(3):
            par[k, place, :] = jnp.broadcast_to(turned[:, 75 + k : 76 + k], (128, 128))
        return carry

    lax.fori_loop(0, N_ROW, source_block, 0)

    def target_block(b, carry):
        for j in range(2):
            rows = target_features(tgt_ref[2 * b + j] * TURNS)
            rows = jnp.concatenate([rows, jnp.zeros((FEATURES - 72, 128), f32)], 0)
            tgt_f[b, :, 128 * j : 128 * j + 128] = rows.astype(bf16)
        return carry

    lax.fori_loop(0, pairs, target_block, 0)

    def distances(b, dest, c):
        place = pl.ds(pl.multiple_of(c * CHUNK, CHUNK), CHUNK)
        dest[place, :] = jnp.dot(src_f[place, :], tgt_f[b], preferred_element_type=f32)

    def prologue(c, carry):
        distances(0, dist_a, c)
        return carry

    lax.fori_loop(0, n_src // CHUNK, prologue, 0)

    def one_pair(b, now, later):
        following = jnp.minimum(b + 1, pairs - 1)

        def step(c, sums):
            sums = list(sums)
            for u in range(CHUNK // 8):
                place = pl.ds(pl.multiple_of(c * CHUNK, CHUNK) + 8 * u, 8)
                eps, amp, phase = [par[k, place, :] for k in range(3)]
                for j in range(2):
                    got = wave(now[place, 128 * j : 128 * j + 128], eps, amp, phase)
                    for m in range(3):
                        sums[3 * j + m] = sums[3 * j + m] + got[m]
            distances(following, later, c)
            return tuple(sums)

        sums = lax.fori_loop(0, n_src // CHUNK, step, tuple(jnp.zeros((8, 128), f32) for _ in range(6)))
        for j in range(2):
            t = 2 * b + j
            weight, part_re, part_im = [jnp.sum(v, axis=0, keepdims=True) for v in sums[3 * j : 3 * j + 3]]
            out_ref[t, 0:1, :] = weight - BACK * part_re + near_re[pl.ds(t, 1), :]
            out_ref[t, 1:2, :] = BACK * part_im + near_im[pl.ds(t, 1), :]

    def two_pairs(b, carry):
        one_pair(2 * b, dist_a, dist_b)
        one_pair(2 * b + 1, dist_b, dist_a)
        return carry

    lax.fori_loop(0, pairs // 2, two_pairs, 0)


def body(positions, area, density, near_dest, near_offset, near_source, near_order):
    panels = positions.shape[1]
    panel_total = panels * N_ROW * N_COL

    targets = jnp.broadcast_to(positions[None], (N_COL, 3, panels))
    targets = lax.all_to_all(targets, COL, 0, 0, tiled=True)

    largest = jnp.max(jnp.abs(density), axis=0)
    safe = jnp.where(largest > 0.0, largest, 1.0)
    ratio = density / safe[None, :]
    size = largest * jnp.sqrt(jnp.sum(ratio * ratio, axis=0))
    phase = jnp.arctan2(density[1], density[0]) * (1.0 / (2.0 * math.pi))
    record = jnp.stack(
        [
            positions[0],
            positions[1],
            positions[2],
            area * (TURNS * TURNS / panel_total),
            area * size * (TURNS / math.sqrt(panel_total)),
            phase,
        ],
        0,
    )
    messages = pl.pallas_call(
        prepare_kernel,
        out_shape=jax.ShapeDtypeStruct((N_ROW, 8, panels), f32),
        in_specs=[VMEM] * 5,
        out_specs=VMEM,
        name="prepare",
    )(
        record,
        near_dest.reshape(4, 128),
        near_offset.reshape(4, 128),
        near_source.reshape(4, 128),
        near_order.reshape(4, 128),
    )
    records = lax.all_to_all(messages, ROW, 0, 0, tiled=True)

    n_src = N_ROW * panels
    partial = pl.pallas_call(
        sum_kernel,
        out_shape=jax.ShapeDtypeStruct((N_COL, 2, panels), f32),
        in_specs=[VMEM] * 2,
        out_specs=VMEM,
        scratch_shapes=[
            pltpu.VMEM((n_src, FEATURES), bf16),
            pltpu.VMEM((N_COL // 2, FEATURES, 256), bf16),
            pltpu.VMEM((3, n_src, 128), f32),
            pltpu.VMEM((N_COL, 128), f32),
            pltpu.VMEM((N_COL, 128), f32),
            pltpu.VMEM((n_src, 256), f32),
            pltpu.VMEM((n_src, 256), f32),
        ],
        compiler_params=pltpu.CompilerParams(vmem_limit_bytes=32 << 20),
        name="pair_sums",
    )(targets, records)
    arrived = lax.all_to_all(partial, COL, 0, 0, tiled=True)
    return 0.5 * density + jnp.sum(arrived, axis=0)


def solution(mesh):
    grid = Mesh(mesh.devices.reshape(2, 16, 2, 2, 4), AXES)
    in_specs = (
        P(None, AXES),
        P(AXES),
        P(None, AXES),
        P(AXES, None),
        P(AXES),
        P(AXES),
        P(AXES),
    )
    return jax.shard_map(body, mesh=grid, in_specs=in_specs, out_specs=P(None, AXES), check_vma=False)
```

```python
import functools
import math

import jax
import jax.numpy as jnp
import numpy as np
from jax import lax
from jax.experimental import pallas as pl
from jax.experimental.pallas import tpu as pltpu
from jax.sharding import Mesh
from jax.sharding import PartitionSpec as P

f32 = jnp.float32
bf16 = jnp.bfloat16
i32 = jnp.int32

AXES = ("xh", "z", "c", "xl", "y")
ROW = ("z",)
COL = ("xh", "c", "xl", "y")
N_ROW, N_COL = 16, 32

TURNS = 6.0 / (2.0 * math.pi)
S1, S3, S5 = 1.57078847, -0.64571199, 0.07766739
B1, B3 = S1 / S5, S3 / S5
ONE = 1.0 / (S5 * S5)
BACK = 8.0 * S5**4

FEATURES = 80
AMP_ROW, PHASE_ROW = 43, 51
CHUNK = 1024
VMEM = pl.BlockSpec(memory_space=pltpu.VMEM)


def wave(s, soft, amp, phase):
    weight = lax.rsqrt(soft) * amp
    s = jnp.maximum(s, 1e-30)
    turns = s * lax.rsqrt(s) + phase
    f = turns - jnp.round(turns)
    f2 = f * f
    sine = f * (B1 + f2 * (B3 + f2))
    u = sine * sine
    d = ONE - u
    rest = weight * d
    return weight, rest * u, (rest * lax.rsqrt(d)) * (sine * ((0.5 * ONE) - u))


def prepare_kernel(rec_ref, dest_ref, off_ref, src_ref, ord_ref, msg_ref):
    for z in range(N_ROW):
        msg_ref[z, 0:6, :] = rec_ref[...]
    dest = dest_ref[...]
    pad = jnp.concatenate([dest, dest], 0).astype(f32)
    columns = jnp.transpose(pad).astype(i32)
    sub = lax.broadcasted_iota(i32, (128, 128), 0)
    lane = lax.broadcasted_iota(i32, (128, 128), 1)
    rows16 = lax.broadcasted_iota(i32, (16, 128), 0)
    first = jnp.zeros((16, 128), f32)
    second = jnp.zeros((16, 128), f32)
    nt = (((1,), (1,)), ((), ()))
    for k in range(4):
        row = dest[k : k + 1, :]
        count = jnp.zeros((128, 128), f32)
        for j in range(k + 1):
            same = columns[:, j : j + 1] == row
            if j == k:
                same = same & (sub < lane)
            count = count + jnp.where(same, 1.0, 0.0)
        rank = jnp.sum(count, axis=0, keepdims=True).astype(i32)
        slot = rank * N_COL + (lax.shift_right_logical(row, 8) * 16 + (row & 15))
        layer = lax.shift_right_logical(row, 4) & 15
        mine = layer == rows16
        low = jnp.where(sub == slot, 1.0, 0.0).astype(bf16)
        high = jnp.where(sub == slot + 64, 1.0, 0.0).astype(bf16)

        def values(ref):
            return jnp.where(mine, ref[k : k + 1, :].astype(f32), 0.0).astype(bf16)

        def put(a, b):
            return lax.dot_general(a, b, nt, preferred_element_type=f32)

        first = first + put(values(off_ref), low) + put(values(src_ref), high)
        second = second + put(values(ord_ref), low)
    msg_ref[:, 6, :] = first
    msg_ref[:, 7, :] = second


def split(x):
    h = jnp.round(x * 64.0) * (1.0 / 64.0)
    m = jnp.round((x - h) * 16384.0) * (1.0 / 16384.0)
    l = jnp.round(((x - h) - m) * 8388608.0) * (1.0 / 8388608.0)
    return h, m, l


def norms(h, m, l):
    exact = jnp.sum(h * h + 2.0 * (h * m), axis=0, keepdims=True)
    e1 = jnp.round(exact * 64.0) * (1.0 / 64.0)
    e2 = jnp.round((exact - e1) * 16384.0) * (1.0 / 16384.0)
    e3 = (exact - e1) - e2
    rest = jnp.sum(2.0 * (h * l) + (m * m + (2.0 * (m * l) + l * l)), axis=0, keepdims=True)
    r1 = jnp.round(rest * 524288.0) * (1.0 / 524288.0)
    r2 = jnp.round((rest - r1) * 134217728.0) * (1.0 / 134217728.0)
    r3 = (rest - r1) - r2
    return (e1, e2, e3), (r1, r2, r3)


def assemble(groups, width):
    blocks = []
    for xyz, extra in groups:
        parts = [xyz]
        if extra is None:
            parts.append(jnp.zeros((5, width), f32))
        else:
            parts.extend(extra)
            parts.append(jnp.zeros((2, width), f32))
        blocks.append(jnp.concatenate(parts, 0))
    return jnp.concatenate(blocks, 0)


def pieces(v):
    first = v.astype(bf16).astype(f32)
    second = (v - first).astype(bf16).astype(f32)
    return [first, second, (v - first) - second]


def source_features(x, eps, amp, phase):
    h, m, l = split(x)
    soft, amp, phase = pieces(eps), pieces(amp), pieces(phase)
    exact, rest = norms(h, m, l)
    ones = [jnp.ones((1, x.shape[1]), f32)] * 3
    order = [
        (h, exact), (h, ones), (m, soft), (m, rest), (h, ones), (l, amp), (m, phase), (l, None), (l, None),
    ]
    return assemble(order, x.shape[1])


def target_features(x, soft):
    h, m, l = split(x)
    exact, rest = norms(h, m, l)
    ones = [jnp.ones((1, x.shape[1]), f32)] * 3
    h, m, l = -2.0 * h, -2.0 * m, -2.0 * l
    last = ones if soft else None
    order = [
        (h, ones), (m, exact), (h, last), (m, ones), (l, rest), (h, None), (l, None), (m, None), (l, None),
    ]
    return assemble(order, x.shape[1])


def near_part(tgt_ref, rec_ref, near_re, near_im):
    src = rec_ref[:, 6, :]
    index = pltpu.roll(src, 64, 1).astype(i32)
    index = jnp.clip(index, 0, 127)
    gathered = [jnp.take_along_axis(rec_ref[:, k, :], index, axis=1) for k in range(6)]
    stack = jnp.concatenate(gathered + [src, rec_ref[:, 7, :]], 0)
    turned = jnp.transpose(stack)[0:64, :]
    fields = [turned] + [pltpu.roll(turned, 128 - 16 * k, 1) for k in range(1, 8)]
    offset = jnp.clip(fields[6].astype(i32), 0, 127)
    s = jnp.zeros((64, 128), f32)
    for k in range(3):
        place = tgt_ref[:, k, :]
        place = jnp.concatenate([place, place], 0)
        gap = jnp.take_along_axis(place, offset, axis=1) * TURNS - fields[k] * TURNS
        s = s + gap * gap
    weight, part_re, part_im = wave(s, s + fields[3], fields[4], fields[5])
    scale = 64.0 * fields[7]
    term_re = scale * (weight - BACK * part_re)
    term_im = scale * (BACK * part_im)
    lane = lax.broadcasted_iota(i32, (64, 128), 1)
    total_re = jnp.zeros((64, 128), f32)
    total_im = jnp.zeros((64, 128), f32)
    for j in range(N_ROW):
        hit = offset[:, j : j + 1] == lane
        total_re = total_re + jnp.where(hit, term_re[:, j : j + 1], 0.0)
        total_im = total_im + jnp.where(hit, term_im[:, j : j + 1], 0.0)
    near_re[...] = total_re[0:32, :] + total_re[32:64, :]
    near_im[...] = total_im[0:32, :] + total_im[32:64, :]


def sum_kernel(tgt_ref, rec_ref, out_ref, src_f, tgt_f, par, near_re, near_im, dist_a, dist_b):
    n_src = N_ROW * 128
    pairs = N_COL // 2

    near_part(tgt_ref, rec_ref, near_re, near_im)

    def source_block(b, carry):
        record = rec_ref[b]
        rows = source_features(record[0:3, :] * TURNS, record[3:4, :], record[4:5, :], record[5:6, :])
        rows = jnp.concatenate([rows, jnp.zeros((FEATURES - 72, 128), f32)], 0)
        place = pl.ds(pl.multiple_of(b * 128, 128), 128)
        src_f[place, :] = jnp.transpose(rows.astype(bf16))
        return carry

    lax.fori_loop(0, N_ROW, source_block, 0, unroll=True)
    row = lax.broadcasted_iota(i32, (FEATURES, 256), 0)
    lane = lax.broadcasted_iota(i32, (FEATURES, 256), 1)
    start = jnp.where(lane < 128, AMP_ROW, PHASE_ROW)
    pick = jnp.where((row >= start) & (row < start + 3), 1.0, 0.0).astype(bf16)

    def columns(c, carry):
        place = pl.ds(pl.multiple_of(c * CHUNK, CHUNK), CHUNK)
        par[place, :] = jnp.dot(src_f[place, :], pick, preferred_element_type=f32)
        return carry

    lax.fori_loop(0, n_src // CHUNK, columns, 0)

    def target_block(b, carry):
        for j in range(2):
            for k in range(2):
                rows = target_features(tgt_ref[2 * b + j] * TURNS, k == 1)
                rows = jnp.concatenate([rows, jnp.zeros((FEATURES - 72, 128), f32)], 0)
                tgt_f[b, :, 256 * k + 128 * j : 256 * k + 128 * j + 128] = rows.astype(bf16)
        return carry

    lax.fori_loop(0, pairs, target_block, 0, unroll=True)

    def distances(b, dest, c):
        place = pl.ds(pl.multiple_of(c * CHUNK, CHUNK), CHUNK)
        dest[place, :] = jnp.dot(src_f[place, :], tgt_f[b], preferred_element_type=f32)

    def prologue(c, carry):
        distances(0, dist_a, c)
        return carry

    lax.fori_loop(0, n_src // CHUNK, prologue, 0)

    def one_pair(b, now, later):
        following = jnp.minimum(b + 1, pairs - 1)

        def step(c, sums):
            sums = list(sums)
            for u in range(CHUNK // 8):
                place = pl.ds(pl.multiple_of(c * CHUNK, CHUNK) + 8 * u, 8)
                amp, phase = par[place, 0:128], par[place, 128:256]
                for j in range(2):
                    lanes = slice(128 * j, 128 * j + 128), slice(256 + 128 * j, 384 + 128 * j)
                    got = wave(now[place, lanes[0]], now[place, lanes[1]], amp, phase)
                    for m in range(3):
                        sums[3 * j + m] = sums[3 * j + m] + got[m]
            distances(following, later, c)
            return tuple(sums)

        sums = lax.fori_loop(0, n_src // CHUNK, step, tuple(jnp.zeros((8, 128), f32) for _ in range(6)))
        for j in range(2):
            t = 2 * b + j
            weight, part_re, part_im = [jnp.sum(v, axis=0, keepdims=True) for v in sums[3 * j : 3 * j + 3]]
            out_ref[t, 0:1, :] = weight - BACK * part_re + near_re[pl.ds(t, 1), :]
            out_ref[t, 1:2, :] = BACK * part_im + near_im[pl.ds(t, 1), :]

    def two_pairs(b, carry):
        one_pair(2 * b, dist_a, dist_b)
        one_pair(2 * b + 1, dist_b, dist_a)
        return carry

    lax.fori_loop(0, pairs // 2, two_pairs, 0)


def body(positions, area, density, near_dest, near_offset, near_source, near_order):
    panels = positions.shape[1]
    panel_total = panels * N_ROW * N_COL

    targets = jnp.broadcast_to(positions[None], (N_COL, 3, panels))
    targets = lax.all_to_all(targets, COL, 0, 0, tiled=True)

    largest = jnp.max(jnp.abs(density), axis=0)
    safe = jnp.where(largest > 0.0, largest, 1.0)
    ratio = density / safe[None, :]
    size = largest * jnp.sqrt(jnp.sum(ratio * ratio, axis=0))
    phase = jnp.arctan2(density[1], density[0]) * (1.0 / (2.0 * math.pi))
    record = jnp.stack(
        [
            positions[0],
            positions[1],
            positions[2],
            area * (TURNS * TURNS / panel_total),
            area * size * (TURNS / math.sqrt(panel_total)),
            phase,
        ],
        0,
    )
    messages = pl.pallas_call(
        prepare_kernel,
        out_shape=jax.ShapeDtypeStruct((N_ROW, 8, panels), f32),
        in_specs=[VMEM] * 5,
        out_specs=VMEM,
        name="prepare",
    )(
        record,
        near_dest.reshape(4, 128),
        near_offset.reshape(4, 128),
        near_source.reshape(4, 128),
        near_order.reshape(4, 128),
    )
    records = lax.all_to_all(messages, ROW, 0, 0, tiled=True)

    n_src = N_ROW * panels
    partial = pl.pallas_call(
        sum_kernel,
        out_shape=jax.ShapeDtypeStruct((N_COL, 2, panels), f32),
        in_specs=[VMEM] * 2,
        out_specs=VMEM,
        scratch_shapes=[
            pltpu.VMEM((n_src, FEATURES), bf16),
            pltpu.VMEM((N_COL // 2, FEATURES, 512), bf16),
            pltpu.VMEM((n_src, 256), f32),
            pltpu.VMEM((N_COL, 128), f32),
            pltpu.VMEM((N_COL, 128), f32),
            pltpu.VMEM((n_src, 512), f32),
            pltpu.VMEM((n_src, 512), f32),
        ],
        compiler_params=pltpu.CompilerParams(vmem_limit_bytes=32 << 20),
        name="pair_sums",
    )(targets, records)
    arrived = lax.all_to_all(partial, COL, 0, 0, tiled=True)
    return 0.5 * density + jnp.sum(arrived, axis=0)


def solution(mesh):
    grid = Mesh(mesh.devices.reshape(2, 16, 2, 2, 4), AXES)
    in_specs = (
        P(None, AXES),
        P(AXES),
        P(None, AXES),
        P(AXES, None),
        P(AXES),
        P(AXES),
        P(AXES),
    )
    return jax.shard_map(body, mesh=grid, in_specs=in_specs, out_specs=P(None, AXES), check_vma=False)
```

```python
import functools
import math

import jax
import jax.numpy as jnp
import numpy as np
from jax import lax
from jax.experimental import pallas as pl
from jax.experimental.pallas import tpu as pltpu
from jax.sharding import Mesh
from jax.sharding import PartitionSpec as P

f32 = jnp.float32
bf16 = jnp.bfloat16
i32 = jnp.int32

AXES = ("xh", "z", "c", "xl", "y")
ROW = ("z",)
COL = ("xh", "c", "xl", "y")
N_ROW, N_COL = 16, 32

TURNS = 6.0 / (2.0 * math.pi)
S1, S3, S5 = 1.57078847, -0.64571199, 0.07766739
B1, B3 = S1 / S5, S3 / S5
ONE = 1.0 / (S5 * S5)
BACK = 8.0 * S5**4

FEATURES = 80
AMP_ROW, PHASE_ROW = 43, 51
CHUNK = 1024
LEAST = 2.0**-39
VMEM = pl.BlockSpec(memory_space=pltpu.VMEM)


def wave(s, soft, amp, phase):
    weight = lax.rsqrt(soft) * amp
    turns = s * lax.rsqrt(s) + phase
    f = turns - jnp.round(turns)
    f2 = f * f
    sine = f * (B1 + f2 * (B3 + f2))
    u = sine * sine
    d = ONE - u
    rest = weight * d
    return weight, rest * u, (rest * lax.rsqrt(d)) * (sine * ((0.5 * ONE) - u))


def prepare_kernel(rec_ref, dest_ref, off_ref, src_ref, ord_ref, msg_ref):
    for z in range(N_ROW):
        msg_ref[z, 0:6, :] = rec_ref[...]
    dest = dest_ref[...]
    pad = jnp.concatenate([dest, dest], 0).astype(f32)
    columns = jnp.transpose(pad).astype(i32)
    sub = lax.broadcasted_iota(i32, (128, 128), 0)
    lane = lax.broadcasted_iota(i32, (128, 128), 1)
    rows16 = lax.broadcasted_iota(i32, (16, 128), 0)
    first = jnp.zeros((16, 128), f32)
    second = jnp.zeros((16, 128), f32)
    nt = (((1,), (1,)), ((), ()))
    for k in range(4):
        row = dest[k : k + 1, :]
        count = jnp.zeros((128, 128), f32)
        for j in range(k + 1):
            same = columns[:, j : j + 1] == row
            if j == k:
                same = same & (sub < lane)
            count = count + jnp.where(same, 1.0, 0.0)
        rank = jnp.sum(count, axis=0, keepdims=True).astype(i32)
        slot = rank * N_COL + (lax.shift_right_logical(row, 8) * 16 + (row & 15))
        layer = lax.shift_right_logical(row, 4) & 15
        mine = layer == rows16
        low = jnp.where(sub == slot, 1.0, 0.0).astype(bf16)
        high = jnp.where(sub == slot + 64, 1.0, 0.0).astype(bf16)

        def values(ref):
            return jnp.where(mine, ref[k : k + 1, :].astype(f32), 0.0).astype(bf16)

        def put(a, b):
            return lax.dot_general(a, b, nt, preferred_element_type=f32)

        first = first + put(values(off_ref), low) + put(values(src_ref), high)
        second = second + put(values(ord_ref), low)
    msg_ref[:, 6, :] = first
    msg_ref[:, 7, :] = second


def split(x):
    h = jnp.round(x * 64.0) * (1.0 / 64.0)
    m = jnp.round((x - h) * 16384.0) * (1.0 / 16384.0)
    l = jnp.round(((x - h) - m) * 8388608.0) * (1.0 / 8388608.0)
    return h, m, l


def grid_pieces(v, first, second):
    a = jnp.round(v * first) * (1.0 / first)
    b = jnp.round((v - a) * second) * (1.0 / second)
    return [a, b, (v - a) - b]


def norms(h, m, l):
    def total(v):
        return jnp.sum(v, axis=0, keepdims=True)

    large = grid_pieces(total(h * h + 2.0 * (h * m)), 2.0**6, 2.0**14)
    middle = grid_pieces(total(2.0 * (h * l) + m * m), 2.0**19, 2.0**27)
    small = grid_pieces(total(2.0 * (m * l) + l * l), 2.0**27, 2.0**35)
    return large, middle, small


def assemble(groups, width):
    blocks = []
    for xyz, extra in groups:
        parts = [xyz] + extra
        parts.append(jnp.zeros((5 - len(extra), width), f32))
        blocks.extend(parts)
    return jnp.concatenate(blocks, 0)


def pieces(v):
    first = v.astype(bf16).astype(f32)
    second = (v - first).astype(bf16).astype(f32)
    return [first, second, (v - first) - second]


def source_features(x, eps, amp, phase):
    h, m, l = split(x)
    soft, amp, phase = pieces(eps), pieces(amp), pieces(phase)
    large, middle, small = norms(h, m, l)
    one = [jnp.ones((1, x.shape[1]), f32)]
    order = [
        (h, large), (h, one * 3), (m, soft),
        (m, middle), (h, one * 3), (l, amp),
        (m, phase), (l, small), (l, one * 4),
    ]
    return assemble(order, x.shape[1])


def target_features(x, soft):
    h, m, l = split(x)
    large, middle, small = norms(h, m, l)
    one = [jnp.ones((1, x.shape[1]), f32)]
    h, m, l = -2.0 * h, -2.0 * m, -2.0 * l
    order = [
        (h, one * 3), (m, large), (h, one * 3 if soft else []),
        (m, one * 3), (l, middle), (h, []),
        (l, []), (m, one * 3), (l, small + ([] if soft else [LEAST * one[0]])),
    ]
    return assemble(order, x.shape[1])


def near_part(tgt_ref, rec_ref, near_re, near_im):
    src = rec_ref[:, 6, :]
    index = pltpu.roll(src, 64, 1).astype(i32)
    index = jnp.clip(index, 0, 127)
    gathered = [jnp.take_along_axis(rec_ref[:, k, :], index, axis=1) for k in range(6)]
    stack = jnp.concatenate(gathered + [src, rec_ref[:, 7, :]], 0)
    turned = jnp.transpose(stack)[0:64, :]
    fields = [turned] + [pltpu.roll(turned, 128 - 16 * k, 1) for k in range(1, 8)]
    offset = jnp.clip(fields[6].astype(i32), 0, 127)
    s = jnp.zeros((64, 128), f32)
    for k in range(3):
        place = tgt_ref[:, k, :]
        place = jnp.concatenate([place, place], 0)
        gap = jnp.take_along_axis(place, offset, axis=1) * TURNS - fields[k] * TURNS
        s = s + gap * gap
    weight, part_re, part_im = wave(jnp.maximum(s, 1e-30), s + fields[3], fields[4], fields[5])
    scale = 64.0 * fields[7]
    term_re = scale * (weight - BACK * part_re)
    term_im = scale * (BACK * part_im)
    lane = lax.broadcasted_iota(i32, (64, 128), 1)
    total_re = jnp.zeros((64, 128), f32)
    total_im = jnp.zeros((64, 128), f32)
    for j in range(N_ROW):
        hit = offset[:, j : j + 1] == lane
        total_re = total_re + jnp.where(hit, term_re[:, j : j + 1], 0.0)
        total_im = total_im + jnp.where(hit, term_im[:, j : j + 1], 0.0)
    near_re[...] = total_re[0:32, :] + total_re[32:64, :]
    near_im[...] = total_im[0:32, :] + total_im[32:64, :]


def sum_kernel(tgt_ref, rec_ref, out_ref, src_f, tgt_f, par, near_re, near_im, dist_a, dist_b):
    n_src = N_ROW * 128
    pairs = N_COL // 2

    near_part(tgt_ref, rec_ref, near_re, near_im)

    def source_block(b, carry):
        record = rec_ref[b]
        rows = source_features(record[0:3, :] * TURNS, record[3:4, :], record[4:5, :], record[5:6, :])
        rows = jnp.concatenate([rows, jnp.zeros((FEATURES - 72, 128), f32)], 0)
        place = pl.ds(pl.multiple_of(b * 128, 128), 128)
        src_f[place, :] = jnp.transpose(rows.astype(bf16))
        return carry

    lax.fori_loop(0, N_ROW, source_block, 0, unroll=True)
    row = lax.broadcasted_iota(i32, (FEATURES, 256), 0)
    lane = lax.broadcasted_iota(i32, (FEATURES, 256), 1)
    start = jnp.where(lane < 128, AMP_ROW, PHASE_ROW)
    pick = jnp.where((row >= start) & (row < start + 3), 1.0, 0.0).astype(bf16)

    for c in range(n_src // CHUNK):
        place = slice(c * CHUNK, c * CHUNK + CHUNK)
        par[place, :] = jnp.dot(src_f[place, :], pick, preferred_element_type=f32)

    def target_block(b, carry):
        for j in range(2):
            for k in range(2):
                rows = target_features(tgt_ref[2 * b + j] * TURNS, k == 1)
                rows = jnp.concatenate([rows, jnp.zeros((FEATURES - 72, 128), f32)], 0)
                tgt_f[b, :, 256 * k + 128 * j : 256 * k + 128 * j + 128] = rows.astype(bf16)
        return carry

    lax.fori_loop(0, pairs, target_block, 0, unroll=True)

    def distances(b, dest, c):
        place = pl.ds(pl.multiple_of(c * CHUNK, CHUNK), CHUNK)
        dest[place, :] = jnp.dot(src_f[place, :], tgt_f[b], preferred_element_type=f32)

    for c in range(n_src // CHUNK):
        distances(0, dist_a, c)

    def one_pair(b, now, later):
        following = jnp.minimum(b + 1, pairs - 1)

        def step(c, sums):
            sums = list(sums)
            for u in range(CHUNK // 8):
                place = pl.ds(pl.multiple_of(c * CHUNK, CHUNK) + 8 * u, 8)
                amp, phase = par[place, 0:128], par[place, 128:256]
                for j in range(2):
                    lanes = slice(128 * j, 128 * j + 128), slice(256 + 128 * j, 384 + 128 * j)
                    got = wave(now[place, lanes[0]], now[place, lanes[1]], amp, phase)
                    for m in range(3):
                        sums[3 * j + m] = sums[3 * j + m] + got[m]
            distances(following, later, c)
            return tuple(sums)

        sums = lax.fori_loop(0, n_src // CHUNK, step, tuple(jnp.zeros((8, 128), f32) for _ in range(6)))
        for j in range(2):
            t = 2 * b + j
            weight, part_re, part_im = [jnp.sum(v, axis=0, keepdims=True) for v in sums[3 * j : 3 * j + 3]]
            out_ref[t, 0:1, :] = weight - BACK * part_re + near_re[pl.ds(t, 1), :]
            out_ref[t, 1:2, :] = BACK * part_im + near_im[pl.ds(t, 1), :]

    def two_pairs(b, carry):
        one_pair(2 * b, dist_a, dist_b)
        one_pair(2 * b + 1, dist_b, dist_a)
        return carry

    lax.fori_loop(0, pairs // 2, two_pairs, 0)


def body(positions, area, density, near_dest, near_offset, near_source, near_order):
    panels = positions.shape[1]
    panel_total = panels * N_ROW * N_COL

    targets = jnp.broadcast_to(positions[None], (N_COL, 3, panels))
    targets = lax.all_to_all(targets, COL, 0, 0, tiled=True)

    largest = jnp.max(jnp.abs(density), axis=0)
    safe = jnp.where(largest > 0.0, largest, 1.0)
    ratio = density / safe[None, :]
    size = largest * jnp.sqrt(jnp.sum(ratio * ratio, axis=0))
    phase = jnp.arctan2(density[1], density[0]) * (1.0 / (2.0 * math.pi))
    record = jnp.stack(
        [
            positions[0],
            positions[1],
            positions[2],
            area * (TURNS * TURNS / panel_total),
            area * size * (TURNS / math.sqrt(panel_total)),
            phase,
        ],
        0,
    )
    messages = pl.pallas_call(
        prepare_kernel,
        out_shape=jax.ShapeDtypeStruct((N_ROW, 8, panels), f32),
        in_specs=[VMEM] * 5,
        out_specs=VMEM,
        name="prepare",
    )(
        record,
        near_dest.reshape(4, 128),
        near_offset.reshape(4, 128),
        near_source.reshape(4, 128),
        near_order.reshape(4, 128),
    )
    records = lax.all_to_all(messages, ROW, 0, 0, tiled=True)

    n_src = N_ROW * panels
    partial = pl.pallas_call(
        sum_kernel,
        out_shape=jax.ShapeDtypeStruct((N_COL, 2, panels), f32),
        in_specs=[VMEM] * 2,
        out_specs=VMEM,
        scratch_shapes=[
            pltpu.VMEM((n_src, FEATURES), bf16),
            pltpu.VMEM((N_COL // 2, FEATURES, 512), bf16),
            pltpu.VMEM((n_src, 256), f32),
            pltpu.VMEM((N_COL, 128), f32),
            pltpu.VMEM((N_COL, 128), f32),
            pltpu.VMEM((n_src, 512), f32),
            pltpu.VMEM((n_src, 512), f32),
        ],
        compiler_params=pltpu.CompilerParams(vmem_limit_bytes=32 << 20),
        name="pair_sums",
    )(targets, records)
    arrived = lax.all_to_all(partial, COL, 0, 0, tiled=True)
    return 0.5 * density + jnp.sum(arrived, axis=0)


def solution(mesh):
    grid = Mesh(mesh.devices.reshape(2, 16, 2, 2, 4), AXES)
    in_specs = (
        P(None, AXES),
        P(AXES),
        P(None, AXES),
        P(AXES, None),
        P(AXES),
        P(AXES),
        P(AXES),
    )
    return jax.shard_map(body, mesh=grid, in_specs=in_specs, out_specs=P(None, AXES), check_vma=False)
```

```python
import functools
import math

import jax
import jax.numpy as jnp
import numpy as np
from jax import lax
from jax.experimental import pallas as pl
from jax.experimental.pallas import tpu as pltpu
from jax.sharding import Mesh
from jax.sharding import PartitionSpec as P

f32 = jnp.float32
bf16 = jnp.bfloat16
i32 = jnp.int32

AXES = ("xh", "z", "c", "xl", "y")
ROW = ("z",)
COL = ("xh", "c", "xl", "y")
N_ROW, N_COL = 16, 32
EARLY = 4

TURNS = 6.0 / (2.0 * math.pi)
S1, S3, S5 = 1.57078847, -0.64571199, 0.07766739
B1, B3 = S1 / S5, S3 / S5
ONE = 1.0 / (S5 * S5)
BACK = 8.0 * S5**4

FEATURES = 80
AMP_ROW, PHASE_ROW = 43, 51
CHUNK = 1024
LEAST = 2.0**-39
VMEM = pl.BlockSpec(memory_space=pltpu.VMEM)


def wave(s, soft, amp, phase):
    weight = lax.rsqrt(soft) * amp
    turns = s * lax.rsqrt(s) + phase
    f = turns - jnp.round(turns)
    f2 = f * f
    sine = f * (B1 + f2 * (B3 + f2))
    u = sine * sine
    d = ONE - u
    rest = weight * d
    return weight, rest * u, (rest * lax.rsqrt(d)) * (sine * ((0.5 * ONE) - u))


def prepare_kernel(rec_ref, dest_ref, off_ref, src_ref, ord_ref, msg_ref):
    for z in range(N_ROW):
        msg_ref[z, 0:6, :] = rec_ref[...]
    dest = dest_ref[...]
    pad = jnp.concatenate([dest, dest], 0).astype(f32)
    columns = jnp.transpose(pad).astype(i32)
    sub = lax.broadcasted_iota(i32, (128, 128), 0)
    lane = lax.broadcasted_iota(i32, (128, 128), 1)
    rows16 = lax.broadcasted_iota(i32, (16, 128), 0)
    first = jnp.zeros((16, 128), f32)
    second = jnp.zeros((16, 128), f32)
    nt = (((1,), (1,)), ((), ()))
    for k in range(4):
        row = dest[k : k + 1, :]
        count = jnp.zeros((128, 128), f32)
        for j in range(k + 1):
            same = columns[:, j : j + 1] == row
            if j == k:
                same = same & (sub < lane)
            count = count + jnp.where(same, 1.0, 0.0)
        rank = jnp.sum(count, axis=0, keepdims=True).astype(i32)
        slot = rank * N_COL + (lax.shift_right_logical(row, 8) * 16 + (row & 15))
        layer = lax.shift_right_logical(row, 4) & 15
        mine = layer == rows16
        low = jnp.where(sub == slot, 1.0, 0.0).astype(bf16)
        high = jnp.where(sub == slot + 64, 1.0, 0.0).astype(bf16)

        def values(ref):
            return jnp.where(mine, ref[k : k + 1, :].astype(f32), 0.0).astype(bf16)

        def put(a, b):
            return lax.dot_general(a, b, nt, preferred_element_type=f32)

        first = first + put(values(off_ref), low) + put(values(src_ref), high)
        second = second + put(values(ord_ref), low)
    msg_ref[:, 6, :] = first
    msg_ref[:, 7, :] = second


def split(x):
    h = jnp.round(x * 64.0) * (1.0 / 64.0)
    m = jnp.round((x - h) * 16384.0) * (1.0 / 16384.0)
    l = jnp.round(((x - h) - m) * 8388608.0) * (1.0 / 8388608.0)
    return h, m, l


def grid_pieces(v, first, second):
    a = jnp.round(v * first) * (1.0 / first)
    b = jnp.round((v - a) * second) * (1.0 / second)
    return [a, b, (v - a) - b]


def norms(h, m, l):
    def total(v):
        return jnp.sum(v, axis=0, keepdims=True)

    large = grid_pieces(total(h * h + 2.0 * (h * m)), 2.0**6, 2.0**14)
    middle = grid_pieces(total(2.0 * (h * l) + m * m), 2.0**19, 2.0**27)
    small = grid_pieces(total(2.0 * (m * l) + l * l), 2.0**27, 2.0**35)
    return large, middle, small


def assemble(groups, width):
    blocks = []
    for xyz, extra in groups:
        parts = [xyz] + extra
        parts.append(jnp.zeros((5 - len(extra), width), f32))
        blocks.extend(parts)
    return jnp.concatenate(blocks, 0)


def pieces(v):
    first = v.astype(bf16).astype(f32)
    second = (v - first).astype(bf16).astype(f32)
    return [first, second, (v - first) - second]


def source_features(x, eps, amp, phase):
    h, m, l = split(x)
    soft, amp, phase = pieces(eps), pieces(amp), pieces(phase)
    large, middle, small = norms(h, m, l)
    one = [jnp.ones((1, x.shape[1]), f32)]
    order = [
        (h, large), (h, one * 3), (m, soft),
        (m, middle), (h, one * 3), (l, amp),
        (m, phase), (l, small), (l, one * 4),
    ]
    return assemble(order, x.shape[1])


def target_features(x, soft):
    h, m, l = split(x)
    large, middle, small = norms(h, m, l)
    one = [jnp.ones((1, x.shape[1]), f32)]
    h, m, l = -2.0 * h, -2.0 * m, -2.0 * l
    order = [
        (h, one * 3), (m, large), (h, one * 3 if soft else []),
        (m, one * 3), (l, middle), (h, []),
        (l, []), (m, one * 3), (l, small + ([] if soft else [LEAST * one[0]])),
    ]
    return assemble(order, x.shape[1])


def near_part(tgt_ref, rec_ref, near_re, near_im):
    src = rec_ref[:, 6, :]
    index = pltpu.roll(src, 64, 1).astype(i32)
    index = jnp.clip(index, 0, 127)
    gathered = [jnp.take_along_axis(rec_ref[:, k, :], index, axis=1) for k in range(6)]
    stack = jnp.concatenate(gathered + [src, rec_ref[:, 7, :]], 0)
    turned = jnp.transpose(stack)[0:64, :]
    fields = [turned] + [pltpu.roll(turned, 128 - 16 * k, 1) for k in range(1, 8)]
    offset = jnp.clip(fields[6].astype(i32), 0, 127)
    s = jnp.zeros((64, 128), f32)
    for k in range(3):
        place = tgt_ref[:, k, :]
        place = jnp.concatenate([place, place], 0)
        gap = jnp.take_along_axis(place, offset, axis=1) * TURNS - fields[k] * TURNS
        s = s + gap * gap
    weight, part_re, part_im = wave(jnp.maximum(s, 1e-30), s + fields[3], fields[4], fields[5])
    scale = 64.0 * fields[7]
    term_re = scale * (weight - BACK * part_re)
    term_im = scale * (BACK * part_im)
    lane = lax.broadcasted_iota(i32, (64, 128), 1)
    total_re = jnp.zeros((64, 128), f32)
    total_im = jnp.zeros((64, 128), f32)
    for j in range(N_ROW):
        hit = offset[:, j : j + 1] == lane
        total_re = total_re + jnp.where(hit, term_re[:, j : j + 1], 0.0)
        total_im = total_im + jnp.where(hit, term_im[:, j : j + 1], 0.0)
    near_re[...] = total_re[0:32, :] + total_re[32:64, :]
    near_im[...] = total_im[0:32, :] + total_im[32:64, :]


def sum_kernel(tgt_ref, rec_ref, out_ref, src_f, tgt_f, par, near_re, near_im, dist_a, dist_b):
    n_src = N_ROW * 128
    pairs = N_COL // 2

    near_part(tgt_ref, rec_ref, near_re, near_im)

    def source_block(b, carry):
        record = rec_ref[b]
        rows = source_features(record[0:3, :] * TURNS, record[3:4, :], record[4:5, :], record[5:6, :])
        rows = jnp.concatenate([rows, jnp.zeros((FEATURES - 72, 128), f32)], 0)
        place = pl.ds(pl.multiple_of(b * 128, 128), 128)
        src_f[place, :] = jnp.transpose(rows.astype(bf16))
        return carry

    lax.fori_loop(0, N_ROW, source_block, 0, unroll=True)
    row = lax.broadcasted_iota(i32, (FEATURES, 256), 0)
    lane = lax.broadcasted_iota(i32, (FEATURES, 256), 1)
    start = jnp.where(lane < 128, AMP_ROW, PHASE_ROW)
    pick = jnp.where((row >= start) & (row < start + 3), 1.0, 0.0).astype(bf16)

    for c in range(n_src // CHUNK):
        place = slice(c * CHUNK, c * CHUNK + CHUNK)
        par[place, :] = jnp.dot(src_f[place, :], pick, preferred_element_type=f32)

    def target_block(b, carry):
        for j in range(2):
            for k in range(2):
                rows = target_features(tgt_ref[2 * b + j] * TURNS, k == 1)
                rows = jnp.concatenate([rows, jnp.zeros((FEATURES - 72, 128), f32)], 0)
                tgt_f[b, :, 256 * k + 128 * j : 256 * k + 128 * j + 128] = rows.astype(bf16)
        return carry

    lax.fori_loop(0, pairs, target_block, 0, unroll=True)

    def distances(b, dest, c):
        place = pl.ds(pl.multiple_of(c * CHUNK, CHUNK), CHUNK)
        dest[place, :] = jnp.dot(src_f[place, :], tgt_f[b], preferred_element_type=f32)

    for c in range(n_src // CHUNK):
        distances(0, dist_a, c)

    def one_pair(b, now, later):
        following = jnp.minimum(b + 1, pairs - 1)

        def step(c, sums):
            sums = list(sums)
            for u in range(CHUNK // 8):
                place = pl.ds(pl.multiple_of(c * CHUNK, CHUNK) + 8 * u, 8)
                amp, phase = par[place, 0:128], par[place, 128:256]
                for j in range(2):
                    lanes = slice(128 * j, 128 * j + 128), slice(256 + 128 * j, 384 + 128 * j)
                    got = wave(now[place, lanes[0]], now[place, lanes[1]], amp, phase)
                    for m in range(3):
                        sums[3 * j + m] = sums[3 * j + m] + got[m]
            distances(following, later, c)
            return tuple(sums)

        sums = lax.fori_loop(0, n_src // CHUNK, step, tuple(jnp.zeros((8, 128), f32) for _ in range(6)))
        for j in range(2):
            t = 2 * b + j
            weight, part_re, part_im = [jnp.sum(v, axis=0, keepdims=True) for v in sums[3 * j : 3 * j + 3]]
            out_ref[t, 0:1, :] = weight - BACK * part_re + near_re[pl.ds(t, 1), :]
            out_ref[t, 1:2, :] = BACK * part_im + near_im[pl.ds(t, 1), :]

    def two_pairs(b, carry):
        one_pair(2 * b, dist_a, dist_b)
        one_pair(2 * b + 1, dist_b, dist_a)
        return carry

    lax.fori_loop(0, pairs // 2, two_pairs, 0)


def body(positions, area, density, near_dest, near_offset, near_source, near_order):
    panels = positions.shape[1]
    panel_total = panels * N_ROW * N_COL

    def gather(v):
        return lax.all_to_all(v, COL, 0, 0, tiled=True)

    def leave(v):
        return v

    early = lax.axis_index("z") < EARLY
    targets = jnp.broadcast_to(positions[None], (N_COL, 3, panels))
    targets = lax.cond(early, gather, leave, targets)

    largest = jnp.max(jnp.abs(density), axis=0)
    safe = jnp.where(largest > 0.0, largest, 1.0)
    ratio = density / safe[None, :]
    size = largest * jnp.sqrt(jnp.sum(ratio * ratio, axis=0))
    phase = jnp.arctan2(density[1], density[0]) * (1.0 / (2.0 * math.pi))
    record = jnp.stack(
        [
            positions[0],
            positions[1],
            positions[2],
            area * (TURNS * TURNS / panel_total),
            area * size * (TURNS / math.sqrt(panel_total)),
            phase,
        ],
        0,
    )
    messages = pl.pallas_call(
        prepare_kernel,
        out_shape=jax.ShapeDtypeStruct((N_ROW, 8, panels), f32),
        in_specs=[VMEM] * 5,
        out_specs=VMEM,
        name="prepare",
    )(
        record,
        near_dest.reshape(4, 128),
        near_offset.reshape(4, 128),
        near_source.reshape(4, 128),
        near_order.reshape(4, 128),
    )
    targets, messages = lax.optimization_barrier((targets, messages))
    records = lax.all_to_all(messages, ROW, 0, 0, tiled=True)
    targets, records = lax.optimization_barrier((targets, records))
    targets = lax.cond(early, leave, gather, targets)

    n_src = N_ROW * panels
    partial = pl.pallas_call(
        sum_kernel,
        out_shape=jax.ShapeDtypeStruct((N_COL, 2, panels), f32),
        in_specs=[VMEM] * 2,
        out_specs=VMEM,
        scratch_shapes=[
            pltpu.VMEM((n_src, FEATURES), bf16),
            pltpu.VMEM((N_COL // 2, FEATURES, 512), bf16),
            pltpu.VMEM((n_src, 256), f32),
            pltpu.VMEM((N_COL, 128), f32),
            pltpu.VMEM((N_COL, 128), f32),
            pltpu.VMEM((n_src, 512), f32),
            pltpu.VMEM((n_src, 512), f32),
        ],
        compiler_params=pltpu.CompilerParams(vmem_limit_bytes=32 << 20),
        name="pair_sums",
    )(targets, records)
    arrived = lax.all_to_all(partial, COL, 0, 0, tiled=True)
    return 0.5 * density + jnp.sum(arrived, axis=0)


def solution(mesh):
    grid = Mesh(mesh.devices.reshape(2, 16, 2, 2, 4), AXES)
    in_specs = (
        P(None, AXES),
        P(AXES),
        P(None, AXES),
        P(AXES, None),
        P(AXES),
        P(AXES),
        P(AXES),
    )
    return jax.shard_map(body, mesh=grid, in_specs=in_specs, out_specs=P(None, AXES), check_vma=False)
```

```python
import functools
import math

import jax
import jax.numpy as jnp
import numpy as np
from jax import lax
from jax.experimental import pallas as pl
from jax.experimental.pallas import tpu as pltpu
from jax.sharding import Mesh
from jax.sharding import PartitionSpec as P

f32 = jnp.float32
bf16 = jnp.bfloat16
i32 = jnp.int32

AXES = ("xh", "z", "c", "xl", "y")
ROW = ("z",)
COL = ("xh", "c", "xl", "y")
N_ROW, N_COL = 16, 32
ORDER = (0, 0, 0, 0, 1, 1, 1, 2, 2, 2, 2, 2, 2, 2, 1, 1)
FIRST, SECOND, N_FIRST = ("y",), ("xh", "c", "xl"), 4

TURNS = 6.0 / (2.0 * math.pi)
S1, S3, S5 = 1.57078847, -0.64571199, 0.07766739
B1, B3 = S1 / S5, S3 / S5
ONE = 1.0 / (S5 * S5)
BACK = 8.0 * S5**4

FEATURES = 80
AMP_ROW, PHASE_ROW = 43, 51
CHUNK = 1024
LEAST = 2.0**-39
VMEM = pl.BlockSpec(memory_space=pltpu.VMEM)


def wave(s, soft, amp, phase):
    weight = lax.rsqrt(soft) * amp
    turns = s * lax.rsqrt(s) + phase
    f = turns - jnp.round(turns)
    f2 = f * f
    sine = f * (B1 + f2 * (B3 + f2))
    u = sine * sine
    d = ONE - u
    rest = weight * d
    return weight, rest * u, (rest * lax.rsqrt(d)) * (sine * ((0.5 * ONE) - u))


def prepare_kernel(pos, area, den, dest_ref, off_ref, src_ref, ord_ref, msg_ref, rep_ref):
    real, imag = den[0:1, :], den[1:2, :]
    largest = jnp.maximum(jnp.abs(real), jnp.abs(imag))
    safe = jnp.where(largest > 0.0, largest, 1.0)
    real_part, imag_part = real / safe, imag / safe
    size = largest * jnp.sqrt(real_part * real_part + imag_part * imag_part)
    phase = jnp.arctan2(imag, real) * (1.0 / (2.0 * math.pi))
    total = 128 * N_ROW * N_COL
    record = jnp.concatenate(
        [
            pos[...],
            area[...] * (TURNS * TURNS / total),
            area[...] * size * (TURNS / math.sqrt(total)),
            phase,
        ],
        0,
    )
    for z in range(N_ROW):
        msg_ref[z, 0:6, :] = record
    for t in range(N_COL):
        rep_ref[t] = pos[...]
    dest = dest_ref[...]
    pad = jnp.concatenate([dest, dest], 0).astype(f32)
    columns = jnp.transpose(pad).astype(i32)
    sub = lax.broadcasted_iota(i32, (128, 128), 0)
    lane = lax.broadcasted_iota(i32, (128, 128), 1)
    rows16 = lax.broadcasted_iota(i32, (16, 128), 0)
    first = jnp.zeros((16, 128), f32)
    second = jnp.zeros((16, 128), f32)
    nt = (((1,), (1,)), ((), ()))
    for k in range(4):
        row = dest[k : k + 1, :]
        count = jnp.zeros((128, 128), f32)
        for j in range(k + 1):
            same = columns[:, j : j + 1] == row
            if j == k:
                same = same & (sub < lane)
            count = count + jnp.where(same, 1.0, 0.0)
        rank = jnp.sum(count, axis=0, keepdims=True).astype(i32)
        slot = rank * N_COL + (lax.shift_right_logical(row, 8) * 16 + (row & 15))
        layer = lax.shift_right_logical(row, 4) & 15
        mine = layer == rows16
        low = jnp.where(sub == slot, 1.0, 0.0).astype(bf16)
        high = jnp.where(sub == slot + 64, 1.0, 0.0).astype(bf16)

        def values(ref):
            return jnp.where(mine, ref[k : k + 1, :].astype(f32), 0.0).astype(bf16)

        def put(a, b):
            return lax.dot_general(a, b, nt, preferred_element_type=f32)

        first = first + put(values(off_ref), low) + put(values(src_ref), high)
        second = second + put(values(ord_ref), low)
    msg_ref[:, 6, :] = first
    msg_ref[:, 7, :] = second


def split(x):
    h = jnp.round(x * 64.0) * (1.0 / 64.0)
    m = jnp.round((x - h) * 16384.0) * (1.0 / 16384.0)
    l = jnp.round(((x - h) - m) * 8388608.0) * (1.0 / 8388608.0)
    return h, m, l


def grid_pieces(v, first, second):
    a = jnp.round(v * first) * (1.0 / first)
    b = jnp.round((v - a) * second) * (1.0 / second)
    return [a, b, (v - a) - b]


def norms(h, m, l):
    def total(v):
        return jnp.sum(v, axis=0, keepdims=True)

    large = grid_pieces(total(h * h + 2.0 * (h * m)), 2.0**6, 2.0**14)
    middle = grid_pieces(total(2.0 * (h * l) + m * m), 2.0**19, 2.0**27)
    small = grid_pieces(total(2.0 * (m * l) + l * l), 2.0**27, 2.0**35)
    return large, middle, small


def assemble(groups, width):
    blocks = []
    for xyz, extra in groups:
        parts = [xyz] + extra
        parts.append(jnp.zeros((5 - len(extra), width), f32))
        blocks.extend(parts)
    return jnp.concatenate(blocks, 0)


def pieces(v):
    first = v.astype(bf16).astype(f32)
    second = (v - first).astype(bf16).astype(f32)
    return [first, second, (v - first) - second]


def source_features(x, eps, amp, phase):
    h, m, l = split(x)
    soft, amp, phase = pieces(eps), pieces(amp), pieces(phase)
    large, middle, small = norms(h, m, l)
    one = [jnp.ones((1, x.shape[1]), f32)]
    order = [
        (h, large), (h, one * 3), (m, soft),
        (m, middle), (h, one * 3), (l, amp),
        (m, phase), (l, small), (l, one * 4),
    ]
    return assemble(order, x.shape[1])


def target_features(x, soft):
    h, m, l = split(x)
    large, middle, small = norms(h, m, l)
    one = [jnp.ones((1, x.shape[1]), f32)]
    h, m, l = -2.0 * h, -2.0 * m, -2.0 * l
    order = [
        (h, one * 3), (m, large), (h, one * 3 if soft else []),
        (m, one * 3), (l, middle), (h, []),
        (l, []), (m, one * 3), (l, small + ([] if soft else [LEAST * one[0]])),
    ]
    return assemble(order, x.shape[1])


def near_part(tgt_ref, rec_ref, near_re, near_im):
    src = rec_ref[:, 6, :]
    index = pltpu.roll(src, 64, 1).astype(i32)
    index = jnp.clip(index, 0, 127)
    gathered = [jnp.take_along_axis(rec_ref[:, k, :], index, axis=1) for k in range(6)]
    stack = jnp.concatenate(gathered + [src, rec_ref[:, 7, :]], 0)
    turned = jnp.transpose(stack)[0:64, :]
    fields = [turned] + [pltpu.roll(turned, 128 - 16 * k, 1) for k in range(1, 8)]
    offset = jnp.clip(fields[6].astype(i32), 0, 127)
    s = jnp.zeros((64, 128), f32)
    for k in range(3):
        place = tgt_ref[:, k, :]
        place = jnp.concatenate([place, place], 0)
        gap = jnp.take_along_axis(place, offset, axis=1) * TURNS - fields[k] * TURNS
        s = s + gap * gap
    weight, part_re, part_im = wave(jnp.maximum(s, 1e-30), s + fields[3], fields[4], fields[5])
    scale = 64.0 * fields[7]
    term_re = scale * (weight - BACK * part_re)
    term_im = scale * (BACK * part_im)
    lane = lax.broadcasted_iota(i32, (64, 128), 1)
    total_re = jnp.zeros((64, 128), f32)
    total_im = jnp.zeros((64, 128), f32)
    for j in range(N_ROW):
        hit = offset[:, j : j + 1] == lane
        total_re = total_re + jnp.where(hit, term_re[:, j : j + 1], 0.0)
        total_im = total_im + jnp.where(hit, term_im[:, j : j + 1], 0.0)
    near_re[...] = total_re[0:32, :] + total_re[32:64, :]
    near_im[...] = total_im[0:32, :] + total_im[32:64, :]


def sum_kernel(tgt_ref, rec_ref, out_ref, src_f, tgt_f, par, near_re, near_im, dist_a, dist_b):
    n_src = N_ROW * 128
    pairs = N_COL // 2

    near_part(tgt_ref, rec_ref, near_re, near_im)

    def source_block(b, carry):
        record = rec_ref[b]
        rows = source_features(record[0:3, :] * TURNS, record[3:4, :], record[4:5, :], record[5:6, :])
        rows = jnp.concatenate([rows, jnp.zeros((FEATURES - 72, 128), f32)], 0)
        place = pl.ds(pl.multiple_of(b * 128, 128), 128)
        src_f[place, :] = jnp.transpose(rows.astype(bf16))
        return carry

    lax.fori_loop(0, N_ROW, source_block, 0, unroll=True)
    row = lax.broadcasted_iota(i32, (FEATURES, 256), 0)
    lane = lax.broadcasted_iota(i32, (FEATURES, 256), 1)
    start = jnp.where(lane < 128, AMP_ROW, PHASE_ROW)
    pick = jnp.where((row >= start) & (row < start + 3), 1.0, 0.0).astype(bf16)

    for c in range(n_src // CHUNK):
        place = slice(c * CHUNK, c * CHUNK + CHUNK)
        par[place, :] = jnp.dot(src_f[place, :], pick, preferred_element_type=f32)

    def target_block(b, carry):
        for j in range(2):
            for k in range(2):
                rows = target_features(tgt_ref[2 * b + j] * TURNS, k == 1)
                rows = jnp.concatenate([rows, jnp.zeros((FEATURES - 72, 128), f32)], 0)
                tgt_f[b, :, 256 * k + 128 * j : 256 * k + 128 * j + 128] = rows.astype(bf16)
        return carry

    lax.fori_loop(0, pairs, target_block, 0, unroll=True)

    def distances(b, dest, c):
        place = pl.ds(pl.multiple_of(c * CHUNK, CHUNK), CHUNK)
        dest[place, :] = jnp.dot(src_f[place, :], tgt_f[b], preferred_element_type=f32)

    for c in range(n_src // CHUNK):
        distances(0, dist_a, c)

    def one_pair(b, now, later):
        following = jnp.minimum(b + 1, pairs - 1)

        def step(c, sums):
            sums = list(sums)
            for u in range(CHUNK // 8):
                place = pl.ds(pl.multiple_of(c * CHUNK, CHUNK) + 8 * u, 8)
                amp, phase = par[place, 0:128], par[place, 128:256]
                for j in range(2):
                    lanes = slice(128 * j, 128 * j + 128), slice(256 + 128 * j, 384 + 128 * j)
                    got = wave(now[place, lanes[0]], now[place, lanes[1]], amp, phase)
                    for m in range(3):
                        sums[3 * j + m] = sums[3 * j + m] + got[m]
            distances(following, later, c)
            return tuple(sums)

        sums = lax.fori_loop(0, n_src // CHUNK, step, tuple(jnp.zeros((8, 128), f32) for _ in range(6)))
        for j in range(2):
            t = 2 * b + j
            weight, part_re, part_im = [jnp.sum(v, axis=0, keepdims=True) for v in sums[3 * j : 3 * j + 3]]
            out_ref[t, 0:1, :] = weight - BACK * part_re + near_re[pl.ds(t, 1), :]
            out_ref[t, 1:2, :] = BACK * part_im + near_im[pl.ds(t, 1), :]

    def two_pairs(b, carry):
        one_pair(2 * b, dist_a, dist_b)
        one_pair(2 * b + 1, dist_b, dist_a)
        return carry

    lax.fori_loop(0, pairs // 2, two_pairs, 0)


def body(positions, area, density, near_dest, near_offset, near_source, near_order):
    panels = positions.shape[1]

    def prepare():
        return pl.pallas_call(
            prepare_kernel,
            out_shape=(
                jax.ShapeDtypeStruct((N_ROW, 8, panels), f32),
                jax.ShapeDtypeStruct((N_COL, 3, panels), f32),
            ),
            in_specs=[VMEM] * 7,
            out_specs=(VMEM, VMEM),
            name="prepare",
        )(
            positions,
            area.reshape(1, 128),
            density,
            near_dest.reshape(4, 128),
            near_offset.reshape(4, 128),
            near_source.reshape(4, 128),
            near_order.reshape(4, 128),
        )

    def repeat(v, times):
        return jnp.broadcast_to(v[None], (times,) + v.shape).reshape((-1,) + v.shape[-2:])

    def exchange(v, axes):
        return lax.all_to_all(v, axes, 0, 0, tiled=True)

    def all_before():
        targets = exchange(repeat(positions, N_COL), COL)
        return prepare()[0], targets

    def some_before():
        targets = exchange(repeat(positions, N_FIRST), FIRST)
        return prepare()[0], repeat(targets, N_COL // N_FIRST)

    def none_before():
        return prepare()

    layer = lax.axis_index("z")
    order = jnp.int32(2)
    for z in range(N_ROW):
        if ORDER[z] != 2:
            order = jnp.where(layer == z, ORDER[z], order)
    messages, targets = lax.switch(order, [all_before, some_before, none_before])
    records = exchange(messages, ROW)
    targets, records = lax.optimization_barrier((targets, records))
    targets = lax.switch(
        order, [lambda v: v, lambda v: exchange(v, SECOND), lambda v: exchange(v, COL)], targets
    )

    n_src = N_ROW * panels
    partial = pl.pallas_call(
        sum_kernel,
        out_shape=jax.ShapeDtypeStruct((N_COL, 2, panels), f32),
        in_specs=[VMEM] * 2,
        out_specs=VMEM,
        scratch_shapes=[
            pltpu.VMEM((n_src, FEATURES), bf16),
            pltpu.VMEM((N_COL // 2, FEATURES, 512), bf16),
            pltpu.VMEM((n_src, 256), f32),
            pltpu.VMEM((N_COL, 128), f32),
            pltpu.VMEM((N_COL, 128), f32),
            pltpu.VMEM((n_src, 512), f32),
            pltpu.VMEM((n_src, 512), f32),
        ],
        compiler_params=pltpu.CompilerParams(vmem_limit_bytes=32 << 20),
        name="pair_sums",
    )(targets, records)
    arrived = lax.all_to_all(partial, COL, 0, 0, tiled=True)
    return 0.5 * density + jnp.sum(arrived, axis=0)


def solution(mesh):
    grid = Mesh(mesh.devices.reshape(2, 16, 2, 2, 4), AXES)
    in_specs = (
        P(None, AXES),
        P(AXES),
        P(None, AXES),
        P(AXES, None),
        P(AXES),
        P(AXES),
        P(AXES),
    )
    return jax.shard_map(body, mesh=grid, in_specs=in_specs, out_specs=P(None, AXES), check_vma=False)
```

```python
import functools
import math

import jax
import jax.numpy as jnp
import numpy as np
from jax import lax
from jax.experimental import pallas as pl
from jax.experimental.pallas import tpu as pltpu
from jax.sharding import Mesh
from jax.sharding import PartitionSpec as P

f32 = jnp.float32
bf16 = jnp.bfloat16
i32 = jnp.int32

AXES = ("xh", "z", "c", "xl", "y")
ROW = ("z",)
COL = ("xh", "c", "xl", "y")
N_ROW, N_COL = 16, 32
ORDER = (0, 0, 0, 0, 1, 1, 1, 2, 2, 2, 2, 2, 2, 2, 1, 1)
FIRST, SECOND, N_FIRST = ("y",), ("xh", "c", "xl"), 4

TURNS = 6.0 / (2.0 * math.pi)
S1, S3, S5 = 1.57078847, -0.64571199, 0.07766739
B1, B3 = S1 / S5, S3 / S5
ONE = 1.0 / (S5 * S5)
BACK = 8.0 * S5**4

FEATURES = 80
AMP_ROW, PHASE_ROW = 43, 51
CHUNK = 1024
LEAST = 2.0**-39
VMEM = pl.BlockSpec(memory_space=pltpu.VMEM)


def wave(s, soft, amp, phase):
    weight = lax.rsqrt(soft) * amp
    turns = s * lax.rsqrt(s) + phase
    f = turns - jnp.round(turns)
    f2 = f * f
    sine = f * (B1 + f2 * (B3 + f2))
    u = sine * sine
    d = ONE - u
    rest = weight * d
    return weight, rest * u, (rest * lax.rsqrt(d)) * (sine * ((0.5 * ONE) - u))


def prepare_kernel(pos, area, den, dest_ref, off_ref, src_ref, ord_ref, msg_ref, rep_ref):
    real, imag = den[0:1, :], den[1:2, :]
    largest = jnp.maximum(jnp.abs(real), jnp.abs(imag))
    safe = jnp.where(largest > 0.0, largest, 1.0)
    real_part, imag_part = real / safe, imag / safe
    size = largest * jnp.sqrt(real_part * real_part + imag_part * imag_part)
    phase = jnp.arctan2(imag, real) * (1.0 / (2.0 * math.pi))
    total = 128 * N_ROW * N_COL
    record = jnp.concatenate(
        [
            pos[...],
            area[...] * (TURNS * TURNS / total),
            area[...] * size * (TURNS / math.sqrt(total)),
            phase,
        ],
        0,
    )
    for z in range(N_ROW):
        msg_ref[z, 0:6, :] = record
    for t in range(N_COL):
        rep_ref[t] = pos[...]
    dest = dest_ref[...]
    pad = jnp.concatenate([dest, dest], 0).astype(f32)
    columns = jnp.transpose(pad).astype(i32)
    sub = lax.broadcasted_iota(i32, (128, 128), 0)
    lane = lax.broadcasted_iota(i32, (128, 128), 1)
    rows16 = lax.broadcasted_iota(i32, (16, 128), 0)
    first = jnp.zeros((16, 128), f32)
    second = jnp.zeros((16, 128), f32)
    nt = (((1,), (1,)), ((), ()))
    for k in range(4):
        row = dest[k : k + 1, :]
        count = jnp.zeros((128, 128), f32)
        for j in range(k + 1):
            same = columns[:, j : j + 1] == row
            if j == k:
                same = same & (sub < lane)
            count = count + jnp.where(same, 1.0, 0.0)
        rank = jnp.sum(count, axis=0, keepdims=True).astype(i32)
        slot = rank * N_COL + (lax.shift_right_logical(row, 8) * 16 + (row & 15))
        layer = lax.shift_right_logical(row, 4) & 15
        mine = layer == rows16
        low = jnp.where(sub == slot, 1.0, 0.0).astype(bf16)
        high = jnp.where(sub == slot + 64, 1.0, 0.0).astype(bf16)

        def values(ref):
            return jnp.where(mine, ref[k : k + 1, :].astype(f32), 0.0).astype(bf16)

        def put(a, b):
            return lax.dot_general(a, b, nt, preferred_element_type=f32)

        first = first + put(values(off_ref), low) + put(values(src_ref), high)
        second = second + put(values(ord_ref), low)
    msg_ref[:, 6, :] = first
    msg_ref[:, 7, :] = second


def split(x):
    h = jnp.round(x * 64.0) * (1.0 / 64.0)
    m = jnp.round((x - h) * 16384.0) * (1.0 / 16384.0)
    l = jnp.round(((x - h) - m) * 8388608.0) * (1.0 / 8388608.0)
    return h, m, l


def grid_pieces(v, first, second):
    a = jnp.round(v * first) * (1.0 / first)
    b = jnp.round((v - a) * second) * (1.0 / second)
    return [a, b, (v - a) - b]


def norms(h, m, l):
    def total(v):
        return jnp.sum(v, axis=0, keepdims=True)

    large = grid_pieces(total(h * h + 2.0 * (h * m)), 2.0**6, 2.0**14)
    middle = grid_pieces(total(2.0 * (h * l) + m * m), 2.0**19, 2.0**27)
    small = grid_pieces(total(2.0 * (m * l) + l * l), 2.0**27, 2.0**35)
    return large, middle, small


def numbered_rows():
    return lax.broadcasted_iota(i32, (8, 128), 0)


def with_rows(v, extra):
    row = numbered_rows()
    for n, e in enumerate(extra):
        v = jnp.where(row == 3 + n, e, v)
    return v


def with_ones(v, count):
    row = numbered_rows()
    return v + jnp.where((row >= 3) & (row < 3 + count), 1.0, 0.0)


def pieces(v):
    first = v.astype(bf16).astype(f32)
    second = (v - first).astype(bf16).astype(f32)
    return [first, second, (v - first) - second]


def features(groups):
    blank = jnp.zeros((FEATURES - 8 * len(groups), 128), f32)
    return jnp.concatenate(groups + [blank], 0).astype(bf16)


def source_features(record):
    h, m, l = split(jnp.where(numbered_rows() < 3, record * TURNS, 0.0))
    large, middle, small = norms(h, m, l)
    parts = pieces(record)
    soft, amp, phase = [[p[k : k + 1, :] for p in parts] for k in (3, 4, 5)]
    return features(
        [
            with_rows(h, large), with_ones(h, 3), with_rows(m, soft),
            with_rows(m, middle), with_ones(h, 3), with_rows(l, amp),
            with_rows(m, phase), with_rows(l, small), with_ones(l, 4),
        ]
    )


def target_features(x):
    h, m, l = split(jnp.concatenate([x * TURNS, jnp.zeros((5, 128), f32)], 0))
    large, middle, small = norms(h, m, l)
    h, m, l = -2.0 * h, -2.0 * m, -2.0 * l
    start = [with_ones(h, 3), with_rows(m, large)]
    rest = [with_ones(m, 3), with_rows(l, middle), h, l, with_ones(m, 3)]
    plain = start + [h] + rest + [with_rows(l, small + [LEAST])]
    soft = start + [with_ones(h, 3)] + rest + [with_rows(l, small)]
    return features(plain), features(soft)


def near_part(tgt_ref, rec_ref, near_re, near_im):
    src = rec_ref[:, 6, :]
    index = pltpu.roll(src, 64, 1).astype(i32)
    index = jnp.clip(index, 0, 127)
    gathered = [jnp.take_along_axis(rec_ref[:, k, :], index, axis=1) for k in range(6)]
    stack = jnp.concatenate(gathered + [src, rec_ref[:, 7, :]], 0)
    turned = jnp.transpose(stack)[0:64, :]
    fields = [turned] + [pltpu.roll(turned, 128 - 16 * k, 1) for k in range(1, 8)]
    offset = jnp.clip(fields[6].astype(i32), 0, 127)
    s = jnp.zeros((64, 128), f32)
    for k in range(3):
        place = tgt_ref[:, k, :]
        place = jnp.concatenate([place, place], 0)
        gap = jnp.take_along_axis(place, offset, axis=1) * TURNS - fields[k] * TURNS
        s = s + gap * gap
    weight, part_re, part_im = wave(jnp.maximum(s, 1e-30), s + fields[3], fields[4], fields[5])
    scale = 64.0 * fields[7]
    term_re = scale * (weight - BACK * part_re)
    term_im = scale * (BACK * part_im)
    lane = lax.broadcasted_iota(i32, (64, 128), 1)
    total_re = jnp.zeros((64, 128), f32)
    total_im = jnp.zeros((64, 128), f32)
    for j in range(N_ROW):
        hit = offset[:, j : j + 1] == lane
        total_re = total_re + jnp.where(hit, term_re[:, j : j + 1], 0.0)
        total_im = total_im + jnp.where(hit, term_im[:, j : j + 1], 0.0)
    near_re[...] = total_re[0:32, :] + total_re[32:64, :]
    near_im[...] = total_im[0:32, :] + total_im[32:64, :]


def sum_kernel(tgt_ref, rec_ref, out_ref, src_f, tgt_f, par, near_re, near_im, dist_a, dist_b):
    n_src = N_ROW * 128
    pairs = N_COL // 2

    near_part(tgt_ref, rec_ref, near_re, near_im)

    def source_block(b, carry):
        place = pl.ds(pl.multiple_of(b * 128, 128), 128)
        src_f[place, :] = jnp.transpose(source_features(rec_ref[b]))
        return carry

    lax.fori_loop(0, N_ROW, source_block, 0, unroll=True)
    row = lax.broadcasted_iota(i32, (FEATURES, 256), 0)
    lane = lax.broadcasted_iota(i32, (FEATURES, 256), 1)
    start = jnp.where(lane < 128, AMP_ROW, PHASE_ROW)
    pick = jnp.where((row >= start) & (row < start + 3), 1.0, 0.0).astype(bf16)

    for c in range(n_src // CHUNK):
        place = slice(c * CHUNK, c * CHUNK + CHUNK)
        par[place, :] = jnp.dot(src_f[place, :], pick, preferred_element_type=f32)

    def target_block(b, carry):
        for j in range(2):
            for k, rows in enumerate(target_features(tgt_ref[2 * b + j])):
                tgt_f[b, :, 256 * k + 128 * j : 256 * k + 128 * j + 128] = rows
        return carry

    lax.fori_loop(0, pairs, target_block, 0, unroll=True)

    def distances(b, dest, c):
        place = pl.ds(pl.multiple_of(c * CHUNK, CHUNK), CHUNK)
        dest[place, :] = jnp.dot(src_f[place, :], tgt_f[b], preferred_element_type=f32)

    for c in range(n_src // CHUNK):
        distances(0, dist_a, c)

    def one_pair(b, now, later):
        following = jnp.minimum(b + 1, pairs - 1)

        def step(c, sums):
            sums = list(sums)
            for u in range(CHUNK // 8):
                place = pl.ds(pl.multiple_of(c * CHUNK, CHUNK) + 8 * u, 8)
                amp, phase = par[place, 0:128], par[place, 128:256]
                for j in range(2):
                    lanes = slice(128 * j, 128 * j + 128), slice(256 + 128 * j, 384 + 128 * j)
                    got = wave(now[place, lanes[0]], now[place, lanes[1]], amp, phase)
                    for m in range(3):
                        sums[3 * j + m] = sums[3 * j + m] + got[m]
            distances(following, later, c)
            return tuple(sums)

        sums = lax.fori_loop(0, n_src // CHUNK, step, tuple(jnp.zeros((8, 128), f32) for _ in range(6)))
        for j in range(2):
            t = 2 * b + j
            weight, part_re, part_im = [jnp.sum(v, axis=0, keepdims=True) for v in sums[3 * j : 3 * j + 3]]
            out_ref[t, 0:1, :] = weight - BACK * part_re + near_re[pl.ds(t, 1), :]
            out_ref[t, 1:2, :] = BACK * part_im + near_im[pl.ds(t, 1), :]

    def two_pairs(b, carry):
        one_pair(2 * b, dist_a, dist_b)
        one_pair(2 * b + 1, dist_b, dist_a)
        return carry

    lax.fori_loop(0, pairs // 2, two_pairs, 0)


def body(positions, area, density, near_dest, near_offset, near_source, near_order):
    panels = positions.shape[1]

    def prepare():
        return pl.pallas_call(
            prepare_kernel,
            out_shape=(
                jax.ShapeDtypeStruct((N_ROW, 8, panels), f32),
                jax.ShapeDtypeStruct((N_COL, 3, panels), f32),
            ),
            in_specs=[VMEM] * 7,
            out_specs=(VMEM, VMEM),
            name="prepare",
        )(
            positions,
            area.reshape(1, 128),
            density,
            near_dest.reshape(4, 128),
            near_offset.reshape(4, 128),
            near_source.reshape(4, 128),
            near_order.reshape(4, 128),
        )

    def repeat(v, times):
        return jnp.broadcast_to(v[None], (times,) + v.shape).reshape((-1,) + v.shape[-2:])

    def exchange(v, axes):
        return lax.all_to_all(v, axes, 0, 0, tiled=True)

    def all_before():
        targets = exchange(repeat(positions, N_COL), COL)
        return prepare()[0], targets

    def some_before():
        targets = exchange(repeat(positions, N_FIRST), FIRST)
        return prepare()[0], repeat(targets, N_COL // N_FIRST)

    def none_before():
        return prepare()

    layer = lax.axis_index("z")
    order = jnp.int32(2)
    for z in range(N_ROW):
        if ORDER[z] != 2:
            order = jnp.where(layer == z, ORDER[z], order)
    messages, targets = lax.switch(order, [all_before, some_before, none_before])
    records = exchange(messages, ROW)
    targets, records = lax.optimization_barrier((targets, records))
    targets = lax.switch(
        order, [lambda v: v, lambda v: exchange(v, SECOND), lambda v: exchange(v, COL)], targets
    )

    n_src = N_ROW * panels
    partial = pl.pallas_call(
        sum_kernel,
        out_shape=jax.ShapeDtypeStruct((N_COL, 2, panels), f32),
        in_specs=[VMEM] * 2,
        out_specs=VMEM,
        scratch_shapes=[
            pltpu.VMEM((n_src, FEATURES), bf16),
            pltpu.VMEM((N_COL // 2, FEATURES, 512), bf16),
            pltpu.VMEM((n_src, 256), f32),
            pltpu.VMEM((N_COL, 128), f32),
            pltpu.VMEM((N_COL, 128), f32),
            pltpu.VMEM((n_src, 512), f32),
            pltpu.VMEM((n_src, 512), f32),
        ],
        compiler_params=pltpu.CompilerParams(vmem_limit_bytes=32 << 20),
        name="pair_sums",
    )(targets, records)
    arrived = lax.all_to_all(partial, COL, 0, 0, tiled=True)
    return 0.5 * density + jnp.sum(arrived, axis=0)


def solution(mesh):
    grid = Mesh(mesh.devices.reshape(2, 16, 2, 2, 4), AXES)
    in_specs = (
        P(None, AXES),
        P(AXES),
        P(None, AXES),
        P(AXES, None),
        P(AXES),
        P(AXES),
        P(AXES),
    )
    return jax.shard_map(body, mesh=grid, in_specs=in_specs, out_specs=P(None, AXES), check_vma=False)
```

```python
import functools
import math

import jax
import jax.numpy as jnp
import numpy as np
from jax import lax
from jax.experimental import pallas as pl
from jax.experimental.pallas import tpu as pltpu
from jax.sharding import Mesh
from jax.sharding import PartitionSpec as P

f32 = jnp.float32
bf16 = jnp.bfloat16
i32 = jnp.int32

AXES = ("xh", "z", "c", "xl", "y")
ROW = ("z",)
COL = ("xh", "c", "xl", "y")
N_ROW, N_COL = 16, 32
ORDER = (0, 0, 0, 0, 1, 1, 2, 2, 2, 2, 2, 2, 2, 2, 2, 2)
FIRST, SECOND, N_FIRST = ("y",), ("xh", "c", "xl"), 4

TURNS = 6.0 / (2.0 * math.pi)
S1, S3, S5 = 1.57078847, -0.64571199, 0.07766739
B1, B3 = S1 / S5, S3 / S5
ONE = 1.0 / (S5 * S5)
BACK = 8.0 * S5**4

FEATURES = 80
AMP_ROW, PHASE_ROW = 43, 51
CHUNK = 1024
LEAST = 2.0**-39
VMEM = pl.BlockSpec(memory_space=pltpu.VMEM)


def wave(s, soft, amp, phase):
    weight = lax.rsqrt(soft) * amp
    turns = s * lax.rsqrt(s) + phase
    f = turns - jnp.round(turns)
    f2 = f * f
    sine = f * (B1 + f2 * (B3 + f2))
    u = sine * sine
    d = ONE - u
    rest = weight * d
    return weight, rest * u, (rest * lax.rsqrt(d)) * (sine * ((0.5 * ONE) - u))


def prepare_kernel(pos, area, den, dest_ref, off_ref, src_ref, ord_ref, msg_ref, rep_ref):
    real, imag = den[0:1, :], den[1:2, :]
    largest = jnp.maximum(jnp.abs(real), jnp.abs(imag))
    safe = jnp.where(largest > 0.0, largest, 1.0)
    real_part, imag_part = real / safe, imag / safe
    size = largest * jnp.sqrt(real_part * real_part + imag_part * imag_part)
    phase = jnp.arctan2(imag, real) * (1.0 / (2.0 * math.pi))
    total = 128 * N_ROW * N_COL
    record = jnp.concatenate(
        [
            pos[...],
            area[...] * (TURNS * TURNS / total),
            area[...] * size * (TURNS / math.sqrt(total)),
            phase,
        ],
        0,
    )
    for z in range(N_ROW):
        msg_ref[z, 0:6, :] = record
    for t in range(N_COL):
        rep_ref[t] = pos[...]
    dest = dest_ref[...]
    pad = jnp.concatenate([dest, dest], 0).astype(f32)
    columns = jnp.transpose(pad).astype(i32)
    sub = lax.broadcasted_iota(i32, (128, 128), 0)
    lane = lax.broadcasted_iota(i32, (128, 128), 1)
    rows16 = lax.broadcasted_iota(i32, (16, 128), 0)
    first = jnp.zeros((16, 128), f32)
    second = jnp.zeros((16, 128), f32)
    nt = (((1,), (1,)), ((), ()))
    for k in range(4):
        row = dest[k : k + 1, :]
        count = jnp.zeros((128, 128), f32)
        for j in range(k + 1):
            same = columns[:, j : j + 1] == row
            if j == k:
                same = same & (sub < lane)
            count = count + jnp.where(same, 1.0, 0.0)
        rank = jnp.sum(count, axis=0, keepdims=True).astype(i32)
        slot = rank * N_COL + (lax.shift_right_logical(row, 8) * 16 + (row & 15))
        layer = lax.shift_right_logical(row, 4) & 15
        mine = layer == rows16
        low = jnp.where(sub == slot, 1.0, 0.0).astype(bf16)
        high = jnp.where(sub == slot + 64, 1.0, 0.0).astype(bf16)

        def values(ref):
            return jnp.where(mine, ref[k : k + 1, :].astype(f32), 0.0).astype(bf16)

        def put(a, b):
            return lax.dot_general(a, b, nt, preferred_element_type=f32)

        first = first + put(values(off_ref), low) + put(values(src_ref), high)
        second = second + put(values(ord_ref), low)
    msg_ref[:, 6, :] = first
    msg_ref[:, 7, :] = second


def split(x):
    h = jnp.round(x * 64.0) * (1.0 / 64.0)
    m = jnp.round((x - h) * 16384.0) * (1.0 / 16384.0)
    l = jnp.round(((x - h) - m) * 8388608.0) * (1.0 / 8388608.0)
    return h, m, l


def grid_pieces(v, first, second):
    a = jnp.round(v * first) * (1.0 / first)
    b = jnp.round((v - a) * second) * (1.0 / second)
    return [a, b, (v - a) - b]


def norms(h, m, l):
    def total(v):
        return jnp.sum(v, axis=0, keepdims=True)

    large = grid_pieces(total(h * h + 2.0 * (h * m)), 2.0**6, 2.0**14)
    middle = grid_pieces(total(2.0 * (h * l) + m * m), 2.0**19, 2.0**27)
    small = grid_pieces(total(2.0 * (m * l) + l * l), 2.0**27, 2.0**35)
    return large, middle, small


def numbered_rows():
    return lax.broadcasted_iota(i32, (8, 128), 0)


def with_rows(v, extra):
    row = numbered_rows()
    for n, e in enumerate(extra):
        v = jnp.where(row == 3 + n, e, v)
    return v


def with_ones(v, count):
    row = numbered_rows()
    return v + jnp.where((row >= 3) & (row < 3 + count), 1.0, 0.0)


def pieces(v):
    first = v.astype(bf16).astype(f32)
    second = (v - first).astype(bf16).astype(f32)
    return [first, second, (v - first) - second]


def features(groups):
    blank = jnp.zeros((FEATURES - 8 * len(groups), 128), f32)
    return jnp.concatenate(groups + [blank], 0).astype(bf16)


def source_features(record):
    h, m, l = split(jnp.where(numbered_rows() < 3, record * TURNS, 0.0))
    large, middle, small = norms(h, m, l)
    parts = pieces(record)
    soft, amp, phase = [[p[k : k + 1, :] for p in parts] for k in (3, 4, 5)]
    return features(
        [
            with_rows(h, large), with_ones(h, 3), with_rows(m, soft),
            with_rows(m, middle), with_ones(h, 3), with_rows(l, amp),
            with_rows(m, phase), with_rows(l, small), with_ones(l, 4),
        ]
    )


def target_features(x):
    h, m, l = split(jnp.concatenate([x * TURNS, jnp.zeros((5, 128), f32)], 0))
    large, middle, small = norms(h, m, l)
    h, m, l = -2.0 * h, -2.0 * m, -2.0 * l
    start = [with_ones(h, 3), with_rows(m, large)]
    rest = [with_ones(m, 3), with_rows(l, middle), h, l, with_ones(m, 3)]
    plain = start + [h] + rest + [with_rows(l, small + [LEAST])]
    soft = start + [with_ones(h, 3)] + rest + [with_rows(l, small)]
    return features(plain), features(soft)


def near_part(tgt_ref, rec_ref, near_re, near_im):
    src = rec_ref[:, 6, :]
    index = pltpu.roll(src, 64, 1).astype(i32)
    index = jnp.clip(index, 0, 127)
    gathered = [jnp.take_along_axis(rec_ref[:, k, :], index, axis=1) for k in range(6)]
    stack = jnp.concatenate(gathered + [src, rec_ref[:, 7, :]], 0)
    turned = jnp.transpose(stack)[0:64, :]
    fields = [turned] + [pltpu.roll(turned, 128 - 16 * k, 1) for k in range(1, 8)]
    offset = jnp.clip(fields[6].astype(i32), 0, 127)
    s = jnp.zeros((64, 128), f32)
    for k in range(3):
        place = tgt_ref[:, k, :]
        place = jnp.concatenate([place, place], 0)
        gap = jnp.take_along_axis(place, offset, axis=1) * TURNS - fields[k] * TURNS
        s = s + gap * gap
    weight, part_re, part_im = wave(jnp.maximum(s, 1e-30), s + fields[3], fields[4], fields[5])
    scale = 64.0 * fields[7]
    term_re = scale * (weight - BACK * part_re)
    term_im = scale * (BACK * part_im)
    lane = lax.broadcasted_iota(i32, (64, 128), 1)
    total_re = jnp.zeros((64, 128), f32)
    total_im = jnp.zeros((64, 128), f32)
    for j in range(N_ROW):
        hit = offset[:, j : j + 1] == lane
        total_re = total_re + jnp.where(hit, term_re[:, j : j + 1], 0.0)
        total_im = total_im + jnp.where(hit, term_im[:, j : j + 1], 0.0)
    near_re[...] = total_re[0:32, :] + total_re[32:64, :]
    near_im[...] = total_im[0:32, :] + total_im[32:64, :]


def sum_kernel(tgt_ref, rec_ref, out_ref, src_f, tgt_f, par, near_re, near_im, dist_a, dist_b):
    n_src = N_ROW * 128
    pairs = N_COL // 2

    near_part(tgt_ref, rec_ref, near_re, near_im)

    def source_block(b, carry):
        place = pl.ds(pl.multiple_of(b * 128, 128), 128)
        src_f[place, :] = jnp.transpose(source_features(rec_ref[b]))
        return carry

    lax.fori_loop(0, N_ROW, source_block, 0, unroll=True)
    row = lax.broadcasted_iota(i32, (FEATURES, 256), 0)
    lane = lax.broadcasted_iota(i32, (FEATURES, 256), 1)
    start = jnp.where(lane < 128, AMP_ROW, PHASE_ROW)
    pick = jnp.where((row >= start) & (row < start + 3), 1.0, 0.0).astype(bf16)

    for c in range(n_src // CHUNK):
        place = slice(c * CHUNK, c * CHUNK + CHUNK)
        par[place, :] = jnp.dot(src_f[place, :], pick, preferred_element_type=f32)

    def target_block(b, carry):
        for j in range(2):
            for k, rows in enumerate(target_features(tgt_ref[2 * b + j])):
                tgt_f[b, :, 256 * k + 128 * j : 256 * k + 128 * j + 128] = rows
        return carry

    lax.fori_loop(0, pairs, target_block, 0, unroll=True)

    def distances(b, dest, c):
        place = pl.ds(pl.multiple_of(c * CHUNK, CHUNK), CHUNK)
        dest[place, :] = jnp.dot(src_f[place, :], tgt_f[b], preferred_element_type=f32)

    for c in range(n_src // CHUNK):
        distances(0, dist_a, c)

    def one_pair(b, now, later):
        following = jnp.minimum(b + 1, pairs - 1)

        def step(c, sums):
            sums = list(sums)
            for u in range(CHUNK // 8):
                place = pl.ds(pl.multiple_of(c * CHUNK, CHUNK) + 8 * u, 8)
                amp, phase = par[place, 0:128], par[place, 128:256]
                for j in range(2):
                    lanes = slice(128 * j, 128 * j + 128), slice(256 + 128 * j, 384 + 128 * j)
                    got = wave(now[place, lanes[0]], now[place, lanes[1]], amp, phase)
                    for m in range(3):
                        sums[3 * j + m] = sums[3 * j + m] + got[m]
            distances(following, later, c)
            return tuple(sums)

        sums = lax.fori_loop(0, n_src // CHUNK, step, tuple(jnp.zeros((8, 128), f32) for _ in range(6)))
        for j in range(2):
            t = 2 * b + j
            weight, part_re, part_im = [jnp.sum(v, axis=0, keepdims=True) for v in sums[3 * j : 3 * j + 3]]
            out_ref[t, 0:1, :] = weight - BACK * part_re + near_re[pl.ds(t, 1), :]
            out_ref[t, 1:2, :] = BACK * part_im + near_im[pl.ds(t, 1), :]

    def two_pairs(b, carry):
        one_pair(2 * b, dist_a, dist_b)
        one_pair(2 * b + 1, dist_b, dist_a)
        return carry

    lax.fori_loop(0, pairs // 2, two_pairs, 0)


def body(positions, area, density, near_dest, near_offset, near_source, near_order):
    panels = positions.shape[1]

    def prepare():
        return pl.pallas_call(
            prepare_kernel,
            out_shape=(
                jax.ShapeDtypeStruct((N_ROW, 8, panels), f32),
                jax.ShapeDtypeStruct((N_COL, 3, panels), f32),
            ),
            in_specs=[VMEM] * 7,
            out_specs=(VMEM, VMEM),
            name="prepare",
        )(
            positions,
            area.reshape(1, 128),
            density,
            near_dest.reshape(4, 128),
            near_offset.reshape(4, 128),
            near_source.reshape(4, 128),
            near_order.reshape(4, 128),
        )

    def repeat(v, times):
        return jnp.broadcast_to(v[None], (times,) + v.shape).reshape((-1,) + v.shape[-2:])

    def exchange(v, axes):
        return lax.all_to_all(v, axes, 0, 0, tiled=True)

    def all_before():
        targets = exchange(repeat(positions, N_COL), COL)
        return prepare()[0], targets

    def some_before():
        targets = exchange(repeat(positions, N_FIRST), FIRST)
        return prepare()[0], repeat(targets, N_COL // N_FIRST)

    def none_before():
        return prepare()

    layer = lax.axis_index("z")
    order = jnp.int32(2)
    for z in range(N_ROW):
        if ORDER[z] != 2:
            order = jnp.where(layer == z, ORDER[z], order)
    messages, targets = lax.switch(order, [all_before, some_before, none_before])
    records = exchange(messages, ROW)
    targets, records = lax.optimization_barrier((targets, records))
    targets = lax.switch(
        order, [lambda v: v, lambda v: exchange(v, SECOND), lambda v: exchange(v, COL)], targets
    )

    n_src = N_ROW * panels
    partial = pl.pallas_call(
        sum_kernel,
        out_shape=jax.ShapeDtypeStruct((N_COL, 2, panels), f32),
        in_specs=[VMEM] * 2,
        out_specs=VMEM,
        scratch_shapes=[
            pltpu.VMEM((n_src, FEATURES), bf16),
            pltpu.VMEM((N_COL // 2, FEATURES, 512), bf16),
            pltpu.VMEM((n_src, 256), f32),
            pltpu.VMEM((N_COL, 128), f32),
            pltpu.VMEM((N_COL, 128), f32),
            pltpu.VMEM((n_src, 512), f32),
            pltpu.VMEM((n_src, 512), f32),
        ],
        compiler_params=pltpu.CompilerParams(vmem_limit_bytes=32 << 20),
        name="pair_sums",
    )(targets, records)
    arrived = lax.all_to_all(partial, COL, 0, 0, tiled=True)
    return 0.5 * density + jnp.sum(arrived, axis=0)


def solution(mesh):
    grid = Mesh(mesh.devices.reshape(2, 16, 2, 2, 4), AXES)
    in_specs = (
        P(None, AXES),
        P(AXES),
        P(None, AXES),
        P(AXES, None),
        P(AXES),
        P(AXES),
        P(AXES),
    )
    return jax.shard_map(body, mesh=grid, in_specs=in_specs, out_specs=P(None, AXES), check_vma=False)
```

```python
import functools
import math

import jax
import jax.numpy as jnp
import numpy as np
from jax import lax
from jax.experimental import pallas as pl
from jax.experimental.pallas import tpu as pltpu
from jax.sharding import Mesh
from jax.sharding import PartitionSpec as P

f32 = jnp.float32
bf16 = jnp.bfloat16
i32 = jnp.int32

AXES = ("xh", "z", "c", "xl", "y")
ROW = ("z",)
COL = ("xh", "c", "xl", "y")
N_ROW, N_COL = 16, 32
ORDER = (0, 0, 0, 0, 1, 1, 2, 2, 2, 2, 2, 2, 2, 2, 2, 1)
FIRST, SECOND, N_FIRST = ("y",), ("xh", "c", "xl"), 4

TURNS = 6.0 / (2.0 * math.pi)
S1, S3, S5 = 1.57078847, -0.64571199, 0.07766739
B1, B3 = S1 / S5, S3 / S5
ONE = 1.0 / (S5 * S5)
BACK = 8.0 * S5**4

FEATURES = 80
AMP_ROW, PHASE_ROW = 43, 51
CHUNK = 1024
LEAST = 2.0**-39
VMEM = pl.BlockSpec(memory_space=pltpu.VMEM)


def wave(s, soft, amp, phase):
    weight = lax.rsqrt(soft) * amp
    turns = s * lax.rsqrt(s) + phase
    f = turns - jnp.round(turns)
    f2 = f * f
    sine = f * (B1 + f2 * (B3 + f2))
    u = sine * sine
    d = ONE - u
    rest = weight * d
    return weight, rest * u, (rest * lax.rsqrt(d)) * (sine * ((0.5 * ONE) - u))


def prepare_kernel(pos, area, den, dest_ref, off_ref, src_ref, ord_ref, msg_ref, rep_ref):
    real, imag = den[0:1, :], den[1:2, :]
    largest = jnp.maximum(jnp.abs(real), jnp.abs(imag))
    safe = jnp.where(largest > 0.0, largest, 1.0)
    real_part, imag_part = real / safe, imag / safe
    size = largest * jnp.sqrt(real_part * real_part + imag_part * imag_part)
    phase = jnp.arctan2(imag, real) * (1.0 / (2.0 * math.pi))
    total = 128 * N_ROW * N_COL
    record = jnp.concatenate(
        [
            pos[...],
            area[...] * (TURNS * TURNS / total),
            area[...] * size * (TURNS / math.sqrt(total)),
            phase,
        ],
        0,
    )
    for z in range(N_ROW):
        msg_ref[z, 0:6, :] = record
    for t in range(N_COL):
        rep_ref[t] = pos[...]
    dest = dest_ref[...]
    pad = jnp.concatenate([dest, dest], 0).astype(f32)
    columns = jnp.transpose(pad).astype(i32)
    sub = lax.broadcasted_iota(i32, (128, 128), 0)
    lane = lax.broadcasted_iota(i32, (128, 128), 1)
    rows16 = lax.broadcasted_iota(i32, (16, 128), 0)
    first = jnp.zeros((16, 128), f32)
    second = jnp.zeros((16, 128), f32)
    nt = (((1,), (1,)), ((), ()))
    for k in range(4):
        row = dest[k : k + 1, :]
        count = jnp.zeros((128, 128), f32)
        for j in range(k + 1):
            same = columns[:, j : j + 1] == row
            if j == k:
                same = same & (sub < lane)
            count = count + jnp.where(same, 1.0, 0.0)
        rank = jnp.sum(count, axis=0, keepdims=True).astype(i32)
        slot = rank * N_COL + (lax.shift_right_logical(row, 8) * 16 + (row & 15))
        layer = lax.shift_right_logical(row, 4) & 15
        mine = layer == rows16
        low = jnp.where(sub == slot, 1.0, 0.0).astype(bf16)
        high = jnp.where(sub == slot + 64, 1.0, 0.0).astype(bf16)

        def values(ref):
            return jnp.where(mine, ref[k : k + 1, :].astype(f32), 0.0).astype(bf16)

        def put(a, b):
            return lax.dot_general(a, b, nt, preferred_element_type=f32)

        first = first + put(values(off_ref), low) + put(values(src_ref), high)
        second = second + put(values(ord_ref), low)
    msg_ref[:, 6, :] = first
    msg_ref[:, 7, :] = second


def split(x):
    h = jnp.round(x * 64.0) * (1.0 / 64.0)
    m = jnp.round((x - h) * 16384.0) * (1.0 / 16384.0)
    l = jnp.round(((x - h) - m) * 8388608.0) * (1.0 / 8388608.0)
    return h, m, l


def grid_pieces(v, first, second):
    a = jnp.round(v * first) * (1.0 / first)
    b = jnp.round((v - a) * second) * (1.0 / second)
    return [a, b, (v - a) - b]


def norms(h, m, l):
    def total(v):
        return jnp.sum(v, axis=0, keepdims=True)

    large = grid_pieces(total(h * h + 2.0 * (h * m)), 2.0**6, 2.0**14)
    middle = grid_pieces(total(2.0 * (h * l) + m * m), 2.0**19, 2.0**27)
    small = grid_pieces(total(2.0 * (m * l) + l * l), 2.0**27, 2.0**35)
    return large, middle, small


def numbered_rows():
    return lax.broadcasted_iota(i32, (8, 128), 0)


def with_rows(v, extra):
    row = numbered_rows()
    for n, e in enumerate(extra):
        v = jnp.where(row == 3 + n, e, v)
    return v


def with_ones(v, count):
    row = numbered_rows()
    return v + jnp.where((row >= 3) & (row < 3 + count), 1.0, 0.0)


def pieces(v):
    first = v.astype(bf16).astype(f32)
    second = (v - first).astype(bf16).astype(f32)
    return [first, second, (v - first) - second]


def features(groups):
    blank = jnp.zeros((FEATURES - 8 * len(groups), 128), f32)
    return jnp.concatenate(groups + [blank], 0).astype(bf16)


def source_features(record):
    h, m, l = split(jnp.where(numbered_rows() < 3, record * TURNS, 0.0))
    large, middle, small = norms(h, m, l)
    parts = pieces(record)
    soft, amp, phase = [[p[k : k + 1, :] for p in parts] for k in (3, 4, 5)]
    return features(
        [
            with_rows(h, large), with_ones(h, 3), with_rows(m, soft),
            with_rows(m, middle), with_ones(h, 3), with_rows(l, amp),
            with_rows(m, phase), with_rows(l, small), with_ones(l, 4),
        ]
    )


def target_features(x):
    h, m, l = split(jnp.concatenate([x * TURNS, jnp.zeros((5, 128), f32)], 0))
    large, middle, small = norms(h, m, l)
    h, m, l = -2.0 * h, -2.0 * m, -2.0 * l
    start = [with_ones(h, 3), with_rows(m, large)]
    rest = [with_ones(m, 3), with_rows(l, middle), h, l, with_ones(m, 3)]
    plain = start + [h] + rest + [with_rows(l, small + [LEAST])]
    soft = start + [with_ones(h, 3)] + rest + [with_rows(l, small)]
    return features(plain), features(soft)


def near_part(tgt_ref, rec_ref, near_re, near_im):
    src = rec_ref[:, 6, :]
    index = pltpu.roll(src, 64, 1).astype(i32)
    index = jnp.clip(index, 0, 127)
    gathered = [jnp.take_along_axis(rec_ref[:, k, :], index, axis=1) for k in range(6)]
    stack = jnp.concatenate(gathered + [src, rec_ref[:, 7, :]], 0)
    turned = jnp.transpose(stack)[0:64, :]
    fields = [turned] + [pltpu.roll(turned, 128 - 16 * k, 1) for k in range(1, 8)]
    offset = jnp.clip(fields[6].astype(i32), 0, 127)
    s = jnp.zeros((64, 128), f32)
    for k in range(3):
        place = tgt_ref[:, k, :]
        place = jnp.concatenate([place, place], 0)
        gap = jnp.take_along_axis(place, offset, axis=1) * TURNS - fields[k] * TURNS
        s = s + gap * gap
    weight, part_re, part_im = wave(jnp.maximum(s, 1e-30), s + fields[3], fields[4], fields[5])
    scale = 64.0 * fields[7]
    term_re = scale * (weight - BACK * part_re)
    term_im = scale * (BACK * part_im)
    lane = lax.broadcasted_iota(i32, (64, 128), 1)
    total_re = jnp.zeros((64, 128), f32)
    total_im = jnp.zeros((64, 128), f32)
    for j in range(N_ROW):
        hit = offset[:, j : j + 1] == lane
        total_re = total_re + jnp.where(hit, term_re[:, j : j + 1], 0.0)
        total_im = total_im + jnp.where(hit, term_im[:, j : j + 1], 0.0)
    near_re[...] = total_re[0:32, :] + total_re[32:64, :]
    near_im[...] = total_im[0:32, :] + total_im[32:64, :]


def sum_kernel(tgt_ref, rec_ref, out_ref, src_f, tgt_f, par, near_re, near_im, dist_a, dist_b):
    n_src = N_ROW * 128
    pairs = N_COL // 2

    near_part(tgt_ref, rec_ref, near_re, near_im)

    def source_block(b, carry):
        place = pl.ds(pl.multiple_of(b * 128, 128), 128)
        src_f[place, :] = jnp.transpose(source_features(rec_ref[b]))
        return carry

    lax.fori_loop(0, N_ROW, source_block, 0, unroll=True)
    row = lax.broadcasted_iota(i32, (FEATURES, 256), 0)
    lane = lax.broadcasted_iota(i32, (FEATURES, 256), 1)
    start = jnp.where(lane < 128, AMP_ROW, PHASE_ROW)
    pick = jnp.where((row >= start) & (row < start + 3), 1.0, 0.0).astype(bf16)

    for c in range(n_src // CHUNK):
        place = slice(c * CHUNK, c * CHUNK + CHUNK)
        par[place, :] = jnp.dot(src_f[place, :], pick, preferred_element_type=f32)

    def target_block(b, carry):
        for j in range(2):
            for k, rows in enumerate(target_features(tgt_ref[2 * b + j])):
                tgt_f[b, :, 256 * k + 128 * j : 256 * k + 128 * j + 128] = rows
        return carry

    lax.fori_loop(0, pairs, target_block, 0, unroll=True)

    def distances(b, dest, c):
        place = pl.ds(pl.multiple_of(c * CHUNK, CHUNK), CHUNK)
        dest[place, :] = jnp.dot(src_f[place, :], tgt_f[b], preferred_element_type=f32)

    for c in range(n_src // CHUNK):
        distances(0, dist_a, c)

    def one_pair(b, now, later):
        following = jnp.minimum(b + 1, pairs - 1)

        def step(c, sums):
            sums = list(sums)
            for u in range(CHUNK // 8):
                place = pl.ds(pl.multiple_of(c * CHUNK, CHUNK) + 8 * u, 8)
                amp, phase = par[place, 0:128], par[place, 128:256]
                for j in range(2):
                    lanes = slice(128 * j, 128 * j + 128), slice(256 + 128 * j, 384 + 128 * j)
                    got = wave(now[place, lanes[0]], now[place, lanes[1]], amp, phase)
                    for m in range(3):
                        sums[3 * j + m] = sums[3 * j + m] + got[m]
            distances(following, later, c)
            return tuple(sums)

        sums = lax.fori_loop(0, n_src // CHUNK, step, tuple(jnp.zeros((8, 128), f32) for _ in range(6)))
        for j in range(2):
            t = 2 * b + j
            weight, part_re, part_im = [jnp.sum(v, axis=0, keepdims=True) for v in sums[3 * j : 3 * j + 3]]
            out_ref[t, 0:1, :] = weight - BACK * part_re + near_re[pl.ds(t, 1), :]
            out_ref[t, 1:2, :] = BACK * part_im + near_im[pl.ds(t, 1), :]

    def two_pairs(b, carry):
        one_pair(2 * b, dist_a, dist_b)
        one_pair(2 * b + 1, dist_b, dist_a)
        return carry

    lax.fori_loop(0, pairs // 2, two_pairs, 0)


def body(positions, area, density, near_dest, near_offset, near_source, near_order):
    panels = positions.shape[1]

    def prepare():
        return pl.pallas_call(
            prepare_kernel,
            out_shape=(
                jax.ShapeDtypeStruct((N_ROW, 8, panels), f32),
                jax.ShapeDtypeStruct((N_COL, 3, panels), f32),
            ),
            in_specs=[VMEM] * 7,
            out_specs=(VMEM, VMEM),
            name="prepare",
        )(
            positions,
            area.reshape(1, 128),
            density,
            near_dest.reshape(4, 128),
            near_offset.reshape(4, 128),
            near_source.reshape(4, 128),
            near_order.reshape(4, 128),
        )

    def repeat(v, times):
        return jnp.broadcast_to(v[None], (times,) + v.shape).reshape((-1,) + v.shape[-2:])

    def exchange(v, axes):
        return lax.all_to_all(v, axes, 0, 0, tiled=True)

    def all_before():
        targets = exchange(repeat(positions, N_COL), COL)
        return prepare()[0], targets

    def some_before():
        targets = exchange(repeat(positions, N_FIRST), FIRST)
        return prepare()[0], repeat(targets, N_COL // N_FIRST)

    def none_before():
        return prepare()

    layer = lax.axis_index("z")
    order = jnp.int32(2)
    for z in range(N_ROW):
        if ORDER[z] != 2:
            order = jnp.where(layer == z, ORDER[z], order)
    messages, targets = lax.switch(order, [all_before, some_before, none_before])
    records = exchange(messages, ROW)
    targets, records = lax.optimization_barrier((targets, records))
    targets = lax.switch(
        order, [lambda v: v, lambda v: exchange(v, SECOND), lambda v: exchange(v, COL)], targets
    )

    n_src = N_ROW * panels
    partial = pl.pallas_call(
        sum_kernel,
        out_shape=jax.ShapeDtypeStruct((N_COL, 2, panels), f32),
        in_specs=[VMEM] * 2,
        out_specs=VMEM,
        scratch_shapes=[
            pltpu.VMEM((n_src, FEATURES), bf16),
            pltpu.VMEM((N_COL // 2, FEATURES, 512), bf16),
            pltpu.VMEM((n_src, 256), f32),
            pltpu.VMEM((N_COL, 128), f32),
            pltpu.VMEM((N_COL, 128), f32),
            pltpu.VMEM((n_src, 512), f32),
            pltpu.VMEM((n_src, 512), f32),
        ],
        compiler_params=pltpu.CompilerParams(vmem_limit_bytes=32 << 20),
        name="pair_sums",
    )(targets, records)
    arrived = lax.all_to_all(partial, COL, 0, 0, tiled=True)
    return 0.5 * density + jnp.sum(arrived, axis=0)


def solution(mesh):
    grid = Mesh(mesh.devices.reshape(2, 16, 2, 2, 4), AXES)
    in_specs = (
        P(None, AXES),
        P(AXES),
        P(None, AXES),
        P(AXES, None),
        P(AXES),
        P(AXES),
        P(AXES),
    )
    return jax.shard_map(body, mesh=grid, in_specs=in_specs, out_specs=P(None, AXES), check_vma=False)
```
